512 devices in a mesh: leaf: 128 (over z, x, core), rep: 4 (over y).
Axes of the slice: x: 4, y: 4, z: 16, core: 2. Of those that a mesh axis runs over, the one named last changes fastest.
Arguments:
- ancestors: bfloat16 [3072, 3072], P('leaf', 'rep'), may hold values from -6 to 6
- panels: bfloat16 [128, 1024, 512], P('leaf'), may hold values from -0.1875 to 0.1875
- structure: int32 [128, 4], P('leaf'), may hold values from 0 to 11, as said below
- inverse_diag: float32 [128, 512, 512], P('leaf', 'rep'), may hold values from -6 to 6
Outputs:
- offdiag: bfloat16 [128, 1024, 512], P('leaf', 'rep')
- diag: float32 [128, 512, 512], P('leaf', 'rep')
The draws below stay inside these ranges and needn't reach their ends.
Inputs may be any that keep to these rules, and one draw needn't show every extreme that they name: `structure`: each row holds 4 different ancestor block numbers in increasing order.
All inputs are finite; a program needn't handle non-finite values.
Results may differ from the reference program's by a relative error of at most 0.012.
Values may be sent and summed in bfloat16 or wider, within the bound.
A program may use at most 64 MiB of HBM per device.

```python
import jax
import jax.numpy as jnp
from jax import lax

W = 256
WC = 512
NA = 12
S = 4
CHILDREN = 128
M = 3072


def draw_structure(key, part):
    key = jax.random.fold_in(key, 7)
    scores = jax.random.randint(key, (CHILDREN, NA), 0, 1 << 20) * NA + jnp.arange(NA, dtype=jnp.int32)[None, :]
    order = jnp.argsort(scores, axis=1)
    return jnp.sort(order[:, :S], axis=1).astype(jnp.int32)


def shard_levels(key, extent, pieces, least, largest):
    def one(dim, blocks):
        steps = jax.random.uniform(jax.random.fold_in(jax.random.fold_in(key, 6), dim), (blocks,), jnp.float32, least / len(pieces), largest / len(pieces))
        return jnp.repeat(jnp.exp(steps), extent[dim] // blocks).reshape((-1,) + (1,) * (len(extent) - dim - 1))

    loudness = one(*pieces[0])
    for cut in pieces[1:]:
        loudness = loudness * one(*cut)
    return loudness


def scatter_about(key, dims, scale, most, split=(), kind=jnp.bfloat16):
    array = jax.random.normal(key, dims, jnp.float32) * scale
    if len(split) > 0:
        array = shard_levels(key, dims, split, -0.22, 0.18) * array
    return jnp.clip(array, min=-most, max=most).astype(kind)


def setup_inputs(seed: int = 0) -> dict:
    key_list = jax.random.split(jax.random.key(seed), 5)
    ancestors = scatter_about(key_list[0], (M, M), 1.0, 6.0, ((0, 128), (1, 4)))
    panels = scatter_about(key_list[1], (CHILDREN, S * W, WC), (S * W) ** -0.5, 0.1875, ((0, 128),))
    structure = draw_structure(jax.random.fold_in(key_list[4], 71), 0)
    inverse_diag = scatter_about(key_list[3], (CHILDREN, WC, WC), 1.0, 6.0, ((0, 128), (1, 4)), jnp.float32)
    return dict(ancestors=ancestors, panels=panels, structure=structure, inverse_diag=inverse_diag)


def reference(ancestors, panels, structure, inverse_diag):
    def one_child(packed):
        blocks, panel_rows, inverse = packed
        row_index = (blocks[:, None] * W + jnp.arange(W, dtype=jnp.int32)[None, :]).reshape(-1).astype(jnp.int32)
        selected = jnp.take(jnp.take(ancestors, row_index, axis=0), row_index, axis=1)
        panel_wide = panel_rows.astype(jnp.float32)
        update = -jnp.dot(selected.astype(jnp.float32), panel_wide, preferred_element_type=jnp.float32)
        rounded = update.astype(jnp.bfloat16)
        diagonal_block = inverse - jnp.dot(panel_wide.T, rounded.astype(jnp.float32), preferred_element_type=jnp.float32)
        return rounded, diagonal_block

    offdiag, diag = lax.map(one_child, (structure, panels, inverse_diag))
    return offdiag, diag
```

```python
import jax
import jax.numpy as jnp
from jax import lax
from jax.experimental import pallas as pl
from jax.experimental.pallas import tpu as pltpu
from jax.sharding import PartitionSpec as P

MESH = pl.DeviceIdType.MESH
Z, X, Y, CORES = 16, 4, 4, 2
PLANE = X * Y * CORES
GROUPS = 3
F32, BF16 = jnp.float32, jnp.bfloat16


def kernel(
    anc_ref, struct_ref, panels_hbm, inv_hbm, off_hbm, diag_hbm,
    panels, inv, s0_send, s0_recv, st_send, st_all, st_smem, tiles, stage, picked, lhs, pt,
    off, d_send, d_recv, diag,
    in_sem, out_sem, s0_sems, st_sems, ring_send, ring_recv, pick_sems, d_send_sem, d_recv_sem,
):
    me, y = lax.axis_index("leaf"), lax.axis_index("rep")
    z, x, c = me // 8, (me // 2) % 4, me % 2

    def leaf(zz, xx, cc):
        return (zz * X + xx) * CORES + cc

    get_panels = pltpu.make_async_copy(panels_hbm.at[0], panels, in_sem.at[0])
    get_inv = pltpu.make_async_copy(inv_hbm.at[0], inv, in_sem.at[1])
    get_panels.start()
    get_inv.start()

    barrier = pltpu.get_barrier_semaphore()

    def greet(n, carry):
        there = leaf(z, (x + n // 8) % X, (c + n % 2) % CORES)
        pl.semaphore_signal(barrier, inc=1, device_id=(there, (y + n // 2) % Y), device_id_type=MESH)
        return carry

    lax.fori_loop(1, PLANE, greet, 0)
    up, down = leaf((z + 1) % Z, x, c), leaf((z + Z - 1) % Z, x, c)
    for there in (up, down):
        pl.semaphore_signal(barrier, inc=1, device_id=(there, y), device_id_type=MESH)

    rows = anc_ref[...].astype(F32)
    for h in range(3):
        for k in range(CORES):
            for t in range(3):
                s0_send[h, k, t] = rows[8 * h:8 * h + 8, 256 * t + 128 * k:256 * t + 128 * k + 128]
    lane = lax.broadcasted_iota(jnp.int32, (8, 128), 1)
    blocks = jnp.zeros((8, 128), jnp.int32)
    for q in range(4):
        blocks = jnp.where(lane == q, struct_ref[0, q], blocks)
    slot = 2 * x + c
    st_send[...] = blocks
    st_all[slot] = blocks

    pl.semaphore_wait(barrier, PLANE + 1)

    for h in range(3):
        eighth = 6 * x + 3 * c + h
        group, half = eighth // 2, eighth % 2
        entry, to_x = group // 4, group % 4
        to_y = (3 * z + entry + y) % Y
        for k in range(CORES):
            here = jnp.logical_and(jnp.logical_and(to_x == x, to_y == y), c == k)

            @pl.when(here)
            def _():
                pltpu.make_async_copy(s0_send.at[h, k], s0_recv.at[entry, half], s0_sems.at[1]).start()

            @pl.when(jnp.logical_not(here))
            def _():
                pltpu.make_async_remote_copy(
                    src_ref=s0_send.at[h, k], dst_ref=s0_recv.at[entry, half],
                    send_sem=s0_sems.at[2 + 2 * h + k], recv_sem=s0_sems.at[1],
                    device_id=(leaf(z, to_x, k), to_y), device_id_type=MESH,
                ).start()

    def tell(n, carry):
        pltpu.make_async_remote_copy(
            src_ref=st_send, dst_ref=st_all.at[slot], send_sem=st_sems.at[0], recv_sem=st_sems.at[1],
            device_id=(leaf(z, (x + n // 2) % X, (c + n % 2) % CORES), y), device_id_type=MESH,
        ).start()
        return carry

    lax.fori_loop(1, X * CORES, tell, 0)

    pltpu.make_async_copy(s0_recv, s0_recv, s0_sems.at[1]).wait()
    for e in range(GROUPS):
        for t in range(3):
            both = jnp.concatenate([s0_recv[e, 0, t], s0_recv[e, 1, t]], axis=0)
            tiles[GROUPS * z + e, t] = both.astype(BF16)

    def pass_on(way, step, e):
        origin = (z + Z - step) % Z if way == 0 else (z + step) % Z
        part = tiles.at[GROUPS * origin + e]
        return pltpu.make_async_remote_copy(
            src_ref=part, dst_ref=part, send_sem=ring_send, recv_sem=ring_recv.at[way, step, e],
            device_id=(up if way == 0 else down, y), device_id_type=MESH,
        )

    def arrived(way, step, e):
        part = tiles.at[0]
        pltpu.make_async_copy(part, part, ring_recv.at[way, step, e]).wait()

    for e in range(GROUPS):
        pass_on(0, 0, e).start()
        pass_on(1, 0, e).start()

    get_panels.wait()
    pt[...] = panels[pl.ds(pl.multiple_of(256 * y, 256), 256), :].T
    told = st_all.at[pl.ds(0, X * CORES - 1)]
    pltpu.make_async_copy(told, told, st_sems.at[1]).wait()
    to_smem = pltpu.make_async_copy(st_all, st_smem, in_sem.at[2])
    to_smem.start()

    for step in range(1, Z // 2 - 1):
        for e in range(GROUPS):
            for way in range(2):
                arrived(way, step - 1, e)
                pass_on(way, step, e).start()
    for e in range(GROUPS):
        for way in range(2):
            arrived(way, Z // 2 - 2, e)

            @pl.when(c == way)
            def _():
                pass_on(way, Z // 2 - 1, e).start()

    to_smem.wait()
    for e in range(GROUPS):
        for way in range(2):

            @pl.when(c == way)
            def _():
                arrived(way, Z // 2 - 1, e)

    def pick(n, to_x, to_c, to_y):
        child = 2 * to_x + to_c
        row = st_smem[child, 0, to_y]
        for q in range(4):
            column = st_smem[child, 0, q]
            held = 4 * row + lax.rem(y + 4 - lax.div(column, 3), 4)
            stage[n, q] = tiles[held, lax.rem(column, 3)]

    def send(n, carry):
        to_x, to_c, to_y = (x + n // 8) % X, (c + n % 2) % CORES, (y + n // 2) % Y
        pick(n, to_x, to_c, to_y)
        pltpu.make_async_remote_copy(
            src_ref=stage.at[n], dst_ref=picked.at[c, y, x], send_sem=pick_sems.at[0], recv_sem=pick_sems.at[1],
            device_id=(leaf(z, to_x, to_c), to_y), device_id_type=MESH,
        ).start()
        return carry

    lax.fori_loop(1, PLANE, send, 0)
    pick(0, x, c, y)
    pltpu.make_async_copy(stage.at[0], picked.at[c, y, x], pick_sems.at[1]).start()

    pltpu.make_async_copy(picked, picked, pick_sems.at[1]).wait()

    for q in range(4):
        quarter = lax.div(struct_ref[0, q], 3)
        for k in range(CORES):
            for part in range(4):
                rows64 = picked[k, lax.rem(quarter + part, 4), :, q]
                lhs[64 * part:64 * part + 64, 256 * q + 128 * k:256 * q + 128 * k + 128] = rows64.reshape(64, 128)
    off[...] = (-jnp.dot(lhs[...], panels[...], preferred_element_type=F32)).astype(BF16)
    put_off = pltpu.make_async_copy(off, off_hbm.at[0], out_sem.at[0])
    put_off.start()

    def share(r):
        return jnp.dot(pt[pl.ds(pl.multiple_of(128 * r, 128), 128), :], off[...], preferred_element_type=F32)

    def give(j):
        return pltpu.make_async_remote_copy(
            src_ref=d_send.at[j], dst_ref=d_recv.at[j], send_sem=d_send_sem.at[j], recv_sem=d_recv_sem.at[j],
            device_id=(me, (y + j + 1) % Y), device_id_type=MESH,
        )

    for j in (1, 0, 2):
        d_send[j] = share((y + j + 1) % Y).astype(BF16)
        give(j).start()
    get_inv.wait()
    diag[...] = inv[...] - share(y)
    for j in (0, 2, 1):
        give(j).wait_recv()
        diag[...] -= d_recv[j].astype(F32)
    put_diag = pltpu.make_async_copy(diag, diag_hbm.at[0], out_sem.at[1])
    put_diag.start()

    for h in range(3):
        eighth = 6 * x + 3 * c + h
        group = eighth // 2
        to_y = (3 * z + group // 4 + y) % Y
        for k in range(CORES):
            here = jnp.logical_and(jnp.logical_and(group % 4 == x, to_y == y), c == k)

            @pl.when(jnp.logical_not(here))
            def _():
                pltpu.make_async_copy(s0_send.at[h, k], s0_send.at[h, k], s0_sems.at[2 + 2 * h + k]).wait()

    pltpu.make_async_copy(told, told, st_sems.at[0]).wait()
    passed = tiles.at[pl.ds(0, GROUPS * (Z - 1))]
    pltpu.make_async_copy(passed, passed, ring_send).wait()
    sent = stage.at[pl.ds(0, PLANE - 1)]
    pltpu.make_async_copy(sent, sent, pick_sems.at[0]).wait()
    for j in range(3):
        give(j).wait_send()
    put_off.wait()
    put_diag.wait()


def per_device(ancestors, panels, structure, inverse_diag):
    vmem, smem, dma = pltpu.VMEM, pltpu.SMEM, pltpu.SemaphoreType.DMA
    return pl.pallas_call(
        kernel,
        out_shape=(
            jax.ShapeDtypeStruct((1, 256, 512), BF16),
            jax.ShapeDtypeStruct((1, 128, 512), F32),
        ),
        in_specs=[
            pl.BlockSpec(memory_space=vmem),
            pl.BlockSpec(memory_space=smem),
            pl.BlockSpec(memory_space=pl.ANY),
            pl.BlockSpec(memory_space=pl.ANY),
        ],
        out_specs=(pl.BlockSpec(memory_space=pl.ANY), pl.BlockSpec(memory_space=pl.ANY)),
        scratch_shapes=[
            vmem((1024, 512), BF16),
            vmem((128, 512), F32),
            vmem((3, CORES, 3, 8, 128), F32),
            vmem((GROUPS, 2, 3, 8, 128), F32),
            vmem((8, 128), jnp.int32),
            vmem((X * CORES, 8, 128), jnp.int32),
            smem((X * CORES, 8, 128), jnp.int32),
            vmem((GROUPS * Z, 3, 16, 128), BF16),
            vmem((PLANE, 4, 16, 128), BF16),
            vmem((CORES, Y, X, 4, 16, 128), BF16),
            vmem((256, 1024), BF16),
            vmem((512, 256), BF16),
            vmem((256, 512), BF16),
            vmem((3, 128, 512), BF16),
            vmem((3, 128, 512), BF16),
            vmem((128, 512), F32),
            dma((3,)),
            dma((2,)),
            dma((8,)),
            dma((2,)),
            dma,
            dma((2, Z // 2, GROUPS)),
            dma((2,)),
            dma((3,)),
            dma((3,)),
        ],
        compiler_params=pltpu.CompilerParams(
            collective_id=0, has_side_effects=True, vmem_limit_bytes=32 * 1024 * 1024
        ),
    )(ancestors, structure, panels, inverse_diag)


def solution(mesh):
    return jax.shard_map(
        per_device,
        mesh=mesh,
        in_specs=(P("leaf", "rep"), P("leaf", None, None), P("leaf", None), P("leaf", "rep", None)),
        out_specs=(P("leaf", "rep", None), P("leaf", "rep", None)),
        check_vma=False,
    )
```

```python
import jax
import jax.numpy as jnp
from jax import lax
from jax.experimental import pallas as pl
from jax.experimental.pallas import tpu as pltpu
from jax.sharding import PartitionSpec as P

MESH = pl.DeviceIdType.MESH
Z, X, Y, CORES = 16, 4, 4, 2
PLANE = X * Y * CORES
GROUPS = 3
JUMPS = (5, -5, 1, -1, 0)
SPREAD = ((1, 1), (-1, -1), (5, 1), (-5, -1), (5, -1), (-5, 1), (5, 3), (2, 1), (-2, -1), (6, 1), (-6, -1))
STEPS = sorted({step for _, step in SPREAD} | {-step for _, step in SPREAD})
assert sorted({j % Z for j in JUMPS} | {(a + b) % Z for a, b in SPREAD}) == list(range(Z))
assert len(JUMPS) + len(SPREAD) == Z
F32, BF16 = jnp.float32, jnp.bfloat16


def kernel(
    anc_hbm, struct_ref, panels_hbm, inv_hbm, off, diag,
    anc, panels, inv, s_send, s_all, pieces, st_send, st_all, st_smem, tiles, stage, picked, lhs, pt,
    d_send, d_recv,
    in_sem, swap_sems, s_sems, spread_send, z_recv, st_sems, pick_sems, d_send_sem, d_recv_sem,
):
    me, y = lax.axis_index("leaf"), lax.axis_index("rep")
    z, x, c = me // 8, (me // 2) % 4, me % 2

    def leaf(zz, xx, cc):
        return (zz * X + xx) * CORES + cc

    def along(step):
        return (z + Z + step) % Z

    get_anc = pltpu.make_async_copy(anc_hbm, anc, in_sem.at[3])
    get_panels = pltpu.make_async_copy(panels_hbm.at[0], panels, in_sem.at[0])
    get_inv = pltpu.make_async_copy(inv_hbm.at[0], inv, in_sem.at[1])
    get_anc.start()
    get_panels.start()
    get_inv.start()

    barrier = pltpu.get_barrier_semaphore()

    def greet(n, carry):
        there = leaf(z, (x + n // 8) % X, (c + n % 2) % CORES)
        pl.semaphore_signal(barrier, inc=1, device_id=(there, (y + n // 2) % Y), device_id_type=MESH)
        return carry

    for jump in JUMPS:
        if jump:
            for e in range(GROUPS):
                from_z, group = along(-jump), 4 * e + x
                there = (leaf(from_z, group // 3, c), (y + 3 * (Z - from_z) + 4 - e) % Y)
                pl.semaphore_signal(barrier, inc=1, device_id=there, device_id_type=MESH)
    for step in STEPS:
        pl.semaphore_signal(barrier, inc=1, device_id=(leaf(along(step), x, c), y), device_id_type=MESH)
    lax.fori_loop(1, PLANE, greet, 0)

    lane = lax.broadcasted_iota(jnp.int32, (8, 128), 1)
    blocks = jnp.zeros((8, 128), jnp.int32)
    for q in range(4):
        blocks = jnp.where(lane == q, struct_ref[0, q], blocks)
    slot = 2 * x + c
    st_send[...] = blocks
    st_all[slot] = blocks
    get_anc.wait()
    rows = anc[...].astype(F32)
    for h in range(3):
        for t in range(3):
            first, second = (rows[8 * h:8 * h + 8, 256 * t + 128 * k:256 * t + 128 * k + 128] for k in range(CORES))
            s_send[h, t] = jnp.where(c == 0, second, first)
            s_all[c, h, t] = jnp.where(c == 0, first, second)

    pl.semaphore_wait(barrier, PLANE - 1 + GROUPS * (len(JUMPS) - 1) + len(STEPS))

    swap = pltpu.make_async_remote_copy(
        src_ref=s_send, dst_ref=s_all.at[c], send_sem=swap_sems.at[0], recv_sem=swap_sems.at[1],
        device_id=(leaf(z, x, 1 - c), y), device_id_type=MESH,
    )
    swap.start()

    def tell(n, carry):
        pltpu.make_async_remote_copy(
            src_ref=st_send, dst_ref=st_all.at[slot], send_sem=st_sems.at[0], recv_sem=st_sems.at[1],
            device_id=(leaf(z, (x + n // 2) % X, (c + n % 2) % CORES), y), device_id_type=MESH,
        ).start()
        return carry

    swap.wait_recv()
    for j in range(3):
        for t in range(3):
            both = [s_all[h // 3, h % 3, t] for h in (2 * j, 2 * j + 1)]
            pieces[j, t] = jnp.concatenate(both, axis=0).astype(BF16)

    def owner(j):
        group = 3 * x + j
        entry = group // 4
        return entry, group % 4, (3 * z + entry + y) % Y

    def scatter(j, jump, here):
        entry, to_x, to_y = owner(j)
        landing = tiles.at[GROUPS * z + entry]
        if here:
            return pltpu.make_async_copy(pieces.at[j], landing, z_recv.at[0, entry])
        return pltpu.make_async_remote_copy(
            src_ref=pieces.at[j], dst_ref=landing,
            send_sem=s_sems.at[0] if jump else s_sems.at[1 + j], recv_sem=z_recv.at[jump % Z, entry],
            device_id=(leaf(along(jump), to_x, c), to_y), device_id_type=MESH,
        )

    def stays(j):
        _, to_x, to_y = owner(j)
        return jnp.logical_and(to_x == x, to_y == y)

    for jump in JUMPS:
        for j in range(3):
            if jump:
                scatter(j, jump, False).start()
            else:
                pl.when(stays(j))(lambda: scatter(j, 0, True).start())
                pl.when(jnp.logical_not(stays(j)))(lambda: scatter(j, 0, False).start())
    lax.fori_loop(1, X * CORES, tell, 0)

    get_panels.wait()
    pt[...] = panels[pl.ds(pl.multiple_of(256 * y, 256), 256), :].T
    told = st_all.at[pl.ds(0, X * CORES - 1)]
    pltpu.make_async_copy(told, told, st_sems.at[1]).wait()
    to_smem = pltpu.make_async_copy(st_all, st_smem, in_sem.at[2])
    to_smem.start()

    landed = set()

    def arrived(o, e):
        if (o, e) not in landed:
            landed.add((o, e))
            pltpu.make_async_copy(tiles.at[0], tiles.at[0], z_recv.at[o % Z, e]).wait()

    def pass_on(o, step, e):
        part = tiles.at[GROUPS * along(-o) + e]
        pltpu.make_async_remote_copy(
            src_ref=part, dst_ref=part, send_sem=spread_send, recv_sem=z_recv.at[(o + step) % Z, e],
            device_id=(leaf(along(step), x, c), y), device_id_type=MESH,
        ).start()

    for o, step in SPREAD:
        for e in range(GROUPS):
            if (o + step) % Z == Z // 2:
                arrived(o, e)
                arrived(-o, e)
                pl.when(c == 0)(lambda: pass_on(o, step, e))
                pl.when(c == 1)(lambda: pass_on(-o, -step, e))
            else:
                arrived(o, e)
                pass_on(o, step, e)
    to_smem.wait()
    for o in range(Z):
        o = o if o < Z // 2 else o - Z
        for e in range(GROUPS):
            arrived(o, e)

    def pick(n, to_x, to_c, to_y):
        child = 2 * to_x + to_c
        row = st_smem[child, 0, to_y]
        for q in range(4):
            column = st_smem[child, 0, q]
            held = 4 * row + lax.rem(y + 4 - lax.div(column, 3), 4)
            stage[n, q] = tiles[held, lax.rem(column, 3)]

    def send(n, carry):
        to_x, to_c, to_y = (x + n // 8) % X, (c + n % 2) % CORES, (y + n // 2) % Y
        pick(n, to_x, to_c, to_y)
        pltpu.make_async_remote_copy(
            src_ref=stage.at[n], dst_ref=picked.at[c, y, x], send_sem=pick_sems.at[0], recv_sem=pick_sems.at[1],
            device_id=(leaf(z, to_x, to_c), to_y), device_id_type=MESH,
        ).start()
        return carry

    lax.fori_loop(1, PLANE, send, 0)
    pick(0, x, c, y)
    pltpu.make_async_copy(stage.at[0], picked.at[c, y, x], pick_sems.at[1]).start()

    pltpu.make_async_copy(picked, picked, pick_sems.at[1]).wait()

    for q in range(4):
        quarter = lax.div(struct_ref[0, q], 3)
        for k in range(CORES):
            for part in range(4):
                rows64 = picked[k, lax.rem(quarter + part, 4), :, q]
                lhs[64 * part:64 * part + 64, 256 * q + 128 * k:256 * q + 128 * k + 128] = rows64.reshape(64, 128)
    off[0] = (-jnp.dot(lhs[...], panels[...], preferred_element_type=F32)).astype(BF16)

    def share(r):
        return jnp.dot(pt[pl.ds(pl.multiple_of(128 * r, 128), 128), :], off[0], preferred_element_type=F32)

    def give(j):
        return pltpu.make_async_remote_copy(
            src_ref=d_send.at[j], dst_ref=d_recv.at[j], send_sem=d_send_sem.at[j], recv_sem=d_recv_sem.at[j],
            device_id=(me, (y + j + 1) % Y), device_id_type=MESH,
        )

    for j in (1, 0, 2):
        d_send[j] = share((y + j + 1) % Y).astype(BF16)
        give(j).start()
    get_inv.wait()
    diag[0] = inv[...] - share(y)
    for j in (0, 2, 1):
        give(j).wait_recv()
        diag[0] -= d_recv[j].astype(F32)

    swap.wait_send()
    pltpu.make_async_copy(told, told, st_sems.at[0]).wait()
    for j in range(3):
        pl.when(jnp.logical_not(stays(j)))(lambda: scatter(j, 0, False).wait_send())
    jumped = tiles.at[pl.ds(0, GROUPS * (len(JUMPS) - 1))]
    pltpu.make_async_copy(jumped, jumped, s_sems.at[0]).wait()
    passed = tiles.at[pl.ds(0, GROUPS * len(SPREAD))]
    pltpu.make_async_copy(passed, passed, spread_send).wait()
    sent = stage.at[pl.ds(0, PLANE - 1)]
    pltpu.make_async_copy(sent, sent, pick_sems.at[0]).wait()
    for j in range(3):
        give(j).wait_send()


def per_device(ancestors, panels, structure, inverse_diag):
    vmem, smem, dma = pltpu.VMEM, pltpu.SMEM, pltpu.SemaphoreType.DMA
    return pl.pallas_call(
        kernel,
        out_shape=(
            pltpu.VMEM((1, 256, 512), BF16),
            pltpu.VMEM((1, 128, 512), F32),
        ),
        in_specs=[
            pl.BlockSpec(memory_space=pl.ANY),
            pl.BlockSpec(memory_space=smem),
            pl.BlockSpec(memory_space=pl.ANY),
            pl.BlockSpec(memory_space=pl.ANY),
        ],
        out_specs=(pl.BlockSpec(memory_space=vmem), pl.BlockSpec(memory_space=vmem)),
        scratch_shapes=[
            vmem((24, 768), BF16),
            vmem((1024, 512), BF16),
            vmem((128, 512), F32),
            vmem((3, 3, 8, 128), F32),
            vmem((CORES, 3, 3, 8, 128), F32),
            vmem((3, 3, 16, 128), BF16),
            vmem((8, 128), jnp.int32),
            vmem((X * CORES, 8, 128), jnp.int32),
            smem((X * CORES, 8, 128), jnp.int32),
            vmem((GROUPS * Z, 3, 16, 128), BF16),
            vmem((PLANE, 4, 16, 128), BF16),
            vmem((CORES, Y, X, 4, 16, 128), BF16),
            vmem((256, 1024), BF16),
            vmem((512, 256), BF16),
            vmem((3, 128, 512), BF16),
            vmem((3, 128, 512), BF16),
            dma((4,)),
            dma((2,)),
            dma((4,)),
            dma,
            dma((Z, GROUPS)),
            dma((2,)),
            dma((2,)),
            dma((3,)),
            dma((3,)),
        ],
        compiler_params=pltpu.CompilerParams(
            collective_id=0, has_side_effects=True, vmem_limit_bytes=32 * 1024 * 1024
        ),
    )(*(pltpu.with_memory_space_constraint(a, pltpu.HBM) for a in (ancestors, structure, panels, inverse_diag)))


def solution(mesh):
    return jax.shard_map(
        per_device,
        mesh=mesh,
        in_specs=(P("leaf", "rep"), P("leaf", None, None), P("leaf", None), P("leaf", "rep", None)),
        out_specs=(P("leaf", "rep", None), P("leaf", "rep", None)),
        check_vma=False,
    )
```

```python
import jax
import jax.numpy as jnp
from jax import lax
from jax.experimental import pallas as pl
from jax.experimental.pallas import tpu as pltpu
from jax.sharding import PartitionSpec as P

MESH = pl.DeviceIdType.MESH
Z, X, Y, CORES = 16, 4, 4, 2
PLANE = X * Y * CORES
GROUPS = 3
OWNER = (
    tuple((n // 3, n % 3, n % 3 + 1) for n in range(12)),
    ((0, 0, 0), (1, 0, 0), (3, 0, 0), (2, 0, 0), (0, 1, 0), (1, 2, 1), (1, 1, 0), (2, 1, 2), (2, 2, 3), (0, 2, 1), (3, 1, 2), (3, 2, 3)),
    ((0, 0, 2), (0, 1, 3), (3, 0, 0), (1, 0, 2), (1, 1, 3), (2, 0, 0), (2, 1, 1), (3, 1, 1), (1, 2, 0), (2, 2, 0), (3, 2, 0), (0, 2, 0)),
    tuple((n // 3, n % 3, n % 3 + 1) for n in range(12)),
)
SHIFT = ((1, 1, 1, 1), (0, 0, 2, 2), (0, 0, 0, 0))
PLACE = [[None] * 16 for _ in range(3)]
HELD = [[[None] * 3 for _ in range(X)] for _ in range(4)]
for kind in range(4):
    for n, (at_x, entry, steps) in enumerate(OWNER[kind]):
        block, row_group = divmod(12 * kind + n, 16)
        assert block == (3 * kind + entry) // 4 and steps == (3 * kind + entry + SHIFT[block][at_x]) % 4
        assert HELD[kind][at_x][entry] is None and 4 * steps + at_x not in PLACE[block]
        PLACE[block][row_group] = 4 * steps + at_x
        HELD[kind][at_x][entry] = n, steps
JUMPS = (5, -5, 0)
SPREAD = ((0, 1), (0, -1), (1, 1), (-1, -1), (5, 1), (-5, -1), (5, -1), (-5, 1), (5, 3), (2, 1), (-2, -1), (6, 1), (-6, -1))
STEPS = sorted({step for _, step in SPREAD} | {-step for _, step in SPREAD})
assert sorted({j % Z for j in JUMPS} | {(a + b) % Z for a, b in SPREAD}) == list(range(Z))
assert len(JUMPS) + len(SPREAD) == Z
F32, BF16 = jnp.float32, jnp.bfloat16


def kernel(
    anc_hbm, struct_ref, panels_hbm, inv_hbm, off, diag,
    anc, panels, inv, pieces, st_send, st_all, st_smem, tiles, stage, picked, lhs, placed, pt,
    d_send, d_recv,
    in_sem, s_sems, spread_send, z_recv, st_sems, pick_sems, d_send_sem, d_recv_sem,
):
    me, y = lax.axis_index("leaf"), lax.axis_index("rep")
    z, x, c = me // 8, (me // 2) % 4, me % 2

    def leaf(zz, xx, cc):
        return (zz * X + xx) * CORES + cc

    def along(step):
        return (z + Z + step) % Z

    def by(index, values):
        return sum(jnp.where(index == n, value, 0) for n, value in enumerate(values))

    shifts = [by(x, values) for values in SHIFT]
    owners = by(8 * (z % 4) + 2 * x + c, [
        sum((1 << 6 * j) * (o[0] + 4 * o[1] + 16 * o[2]) for j, o in enumerate(OWNER[kind][g // 2] for g in range(3 * n, 3 * n + 3)))
        for kind in range(4) for n in range(X * CORES)
    ])

    def sources(from_z):
        return by(4 * (from_z % 4) + x, [
            sum((1 << 6 * e) * (n + 16 * steps) for e, (n, steps) in enumerate(HELD[kind][at])) for kind in range(4) for at in range(X)
        ])

    get_anc = pltpu.make_async_copy(anc_hbm, anc, in_sem.at[3])
    get_panels = pltpu.make_async_copy(panels_hbm.at[0], panels, in_sem.at[0])
    get_inv = pltpu.make_async_copy(inv_hbm.at[0], inv, in_sem.at[1])
    get_anc.start()
    get_panels.start()
    get_inv.start()

    barrier = pltpu.get_barrier_semaphore()

    def greet(n, carry):
        there = leaf(z, (x + n // 8) % X, (c + n % 2) % CORES)
        pl.semaphore_signal(barrier, inc=1, device_id=(there, (y + n // 2) % Y), device_id_type=MESH)
        return carry

    for jump in JUMPS:
        if jump:
            held = sources(along(-jump))
            for e in range(GROUPS):
                pair, steps = held // (1 << 6 * e) % 16, held // (1 << 6 * e + 4) % 4
                there = (leaf(along(-jump), pair // 3, (2 * pair + c) // 3 % 2), (y + Y - steps) % Y)
                pl.semaphore_signal(barrier, inc=1, device_id=there, device_id_type=MESH)
    for step in STEPS:
        pl.semaphore_signal(barrier, inc=1, device_id=(leaf(along(step), x, c), y), device_id_type=MESH)
    lax.fori_loop(1, PLANE, greet, 0)

    lane = lax.broadcasted_iota(jnp.int32, (8, 128), 1)
    blocks = jnp.zeros((8, 128), jnp.int32)
    for q in range(4):
        blocks = jnp.where(lane == q, struct_ref[0, q], blocks)
    slot = 2 * x + c
    st_send[...] = blocks
    st_all[slot] = blocks
    get_anc.wait()
    rows = anc[...].astype(F32)
    for h in range(3):
        for t in range(3):
            halves = [rows[8 * h:8 * h + 8, 256 * t + 128 * k:256 * t + 128 * k + 128] for k in range(2)]
            pieces[h, t] = jnp.concatenate(halves, axis=0).astype(BF16)

    pl.semaphore_wait(barrier, PLANE - 1 + GROUPS * (len(JUMPS) - 1) + len(STEPS))

    def tell(n, carry):
        pltpu.make_async_remote_copy(
            src_ref=st_send, dst_ref=st_all.at[slot], send_sem=st_sems.at[0], recv_sem=st_sems.at[1],
            device_id=(leaf(z, (x + n // 2) % X, (c + n % 2) % CORES), y), device_id_type=MESH,
        ).start()
        return carry

    def owner(j):
        one = owners // (1 << 6 * j) % 64
        return one // 4 % 4, one % 4, (y + one // 16) % Y, (3 * c + j) % 2

    def scatter(j, jump, here):
        entry, to_x, to_y, to_c = owner(j)
        landing = tiles.at[GROUPS * z + entry]
        if here:
            return pltpu.make_async_copy(pieces.at[j], landing, z_recv.at[0, entry])
        return pltpu.make_async_remote_copy(
            src_ref=pieces.at[j], dst_ref=landing,
            send_sem=s_sems.at[0] if jump else s_sems.at[1 + j], recv_sem=z_recv.at[jump % Z, entry],
            device_id=(leaf(along(jump), to_x, to_c), to_y), device_id_type=MESH,
        )

    def stays(j):
        _, to_x, to_y, to_c = owner(j)
        return jnp.logical_and(jnp.logical_and(to_x == x, to_y == y), to_c == c)

    for jump in JUMPS:
        for j in range(3):
            if jump:
                scatter(j, jump, False).start()
            else:
                pl.when(stays(j))(lambda: scatter(j, 0, True).start())
                pl.when(jnp.logical_not(stays(j)))(lambda: scatter(j, 0, False).start())
    lax.fori_loop(1, X * CORES, tell, 0)

    landed = set()

    def arrived(o, e):
        if (o, e) not in landed:
            landed.add((o, e))
            pltpu.make_async_copy(tiles.at[0], tiles.at[0], z_recv.at[o % Z, e]).wait()

    def pass_on(o, step, e):
        part = tiles.at[GROUPS * along(-o) + e]
        pltpu.make_async_remote_copy(
            src_ref=part, dst_ref=part, send_sem=spread_send, recv_sem=z_recv.at[(o + step) % Z, e],
            device_id=(leaf(along(step), x, c), y), device_id_type=MESH,
        ).start()

    for o, step in SPREAD:
        for e in range(GROUPS):
            if (o + step) % Z == Z // 2:
                arrived(o, e)
                arrived(-o, e)
                pl.when(c == 0)(lambda: pass_on(o, step, e))
                pl.when(c == 1)(lambda: pass_on(-o, -step, e))
            else:
                arrived(o, e)
                pass_on(o, step, e)
    get_panels.wait()
    pt[...] = panels[pl.ds(pl.multiple_of(256 * y, 256), 256), :].T
    told = st_all.at[pl.ds(0, X * CORES - 1)]
    pltpu.make_async_copy(told, told, st_sems.at[1]).wait()
    to_smem = pltpu.make_async_copy(st_all, st_smem, in_sem.at[2])
    to_smem.start()
    for o in range(Z):
        o = o if o < Z // 2 else o - Z
        for e in range(GROUPS):
            arrived(o, e)
    to_smem.wait()

    def pick(n, to_x, to_c, to_y):
        child = 2 * to_x + to_c
        row = st_smem[child, 0, to_y]
        shift = by(lax.rem(row, 3), shifts)
        for q in range(4):
            column = st_smem[child, 0, q]
            held = 4 * row + lax.rem(y + 8 - shift - lax.div(column, 3), 4)
            stage[n, q] = tiles[held, lax.rem(column, 3)]

    def send(n, carry):
        to_x, to_c, to_y = (x + n // 8) % X, (c + n % 2) % CORES, (y + n // 2) % Y
        pick(n, to_x, to_c, to_y)
        pltpu.make_async_remote_copy(
            src_ref=stage.at[n], dst_ref=picked.at[c, y, x], send_sem=pick_sems.at[0], recv_sem=pick_sems.at[1],
            device_id=(leaf(z, to_x, to_c), to_y), device_id_type=MESH,
        ).start()
        return carry

    lax.fori_loop(1, PLANE, send, 0)
    pick(0, x, c, y)
    pltpu.make_async_copy(stage.at[0], picked.at[c, y, x], pick_sems.at[1]).start()

    pltpu.make_async_copy(picked, picked, pick_sems.at[1]).wait()

    for q in range(4):
        quarter = lax.div(struct_ref[0, q], 3)
        for part in range(4):
            pair = [picked[k, lax.rem(quarter + part, 4), :, q].astype(F32).reshape(X, 2, 8, 128) for k in range(CORES)]
            for k in range(2):
                rows64 = jnp.concatenate([pair[0][:, k], pair[1][:, k]], axis=1).astype(BF16).reshape(64, 128)
                lhs[64 * part:64 * part + 64, 256 * q + 128 * k:256 * q + 128 * k + 128] = rows64
    update = (-jnp.dot(lhs[...], panels[...], preferred_element_type=F32)).astype(BF16)
    placed[...] = update.reshape(16, 16, 512)
    kind = lax.rem(by(y, [struct_ref[0, q] for q in range(4)]), 3)
    for first in range(0, 16, 4):
        places = by(kind, [sum(PLACE[n][first + m] << 4 * m for m in range(4)) for n in range(3)])
        for m in range(4):
            off[0, 16 * (first + m):16 * (first + m) + 16] = placed[lax.rem(lax.div(places, 1 << 4 * m), 16)]

    def share(r):
        return jnp.dot(pt[pl.ds(pl.multiple_of(128 * r, 128), 128), :], off[0], preferred_element_type=F32)

    def give(j):
        return pltpu.make_async_remote_copy(
            src_ref=d_send.at[j], dst_ref=d_recv.at[j], send_sem=d_send_sem.at[j], recv_sem=d_recv_sem.at[j],
            device_id=(me, (y + j + 1) % Y), device_id_type=MESH,
        )

    for j in (1, 0, 2):
        d_send[j] = share((y + j + 1) % Y).astype(BF16)
        give(j).start()
    get_inv.wait()
    diag[0] = inv[...] - share(y)
    for j in (0, 2, 1):
        give(j).wait_recv()
        diag[0] -= d_recv[j].astype(F32)

    pltpu.make_async_copy(told, told, st_sems.at[0]).wait()
    for j in range(3):
        pl.when(jnp.logical_not(stays(j)))(lambda: scatter(j, 0, False).wait_send())
    jumped = tiles.at[pl.ds(0, GROUPS * (len(JUMPS) - 1))]
    pltpu.make_async_copy(jumped, jumped, s_sems.at[0]).wait()
    passed = tiles.at[pl.ds(0, GROUPS * len(SPREAD))]
    pltpu.make_async_copy(passed, passed, spread_send).wait()
    sent = stage.at[pl.ds(0, PLANE - 1)]
    pltpu.make_async_copy(sent, sent, pick_sems.at[0]).wait()
    for j in range(3):
        give(j).wait_send()


def per_device(ancestors, panels, structure, inverse_diag):
    vmem, smem, dma = pltpu.VMEM, pltpu.SMEM, pltpu.SemaphoreType.DMA
    return pl.pallas_call(
        kernel,
        out_shape=(
            pltpu.VMEM((1, 256, 512), BF16),
            pltpu.VMEM((1, 128, 512), F32),
        ),
        in_specs=[
            pl.BlockSpec(memory_space=pl.ANY),
            pl.BlockSpec(memory_space=smem),
            pl.BlockSpec(memory_space=pl.ANY),
            pl.BlockSpec(memory_space=pl.ANY),
        ],
        out_specs=(pl.BlockSpec(memory_space=vmem), pl.BlockSpec(memory_space=vmem)),
        scratch_shapes=[
            vmem((24, 768), BF16),
            vmem((1024, 512), BF16),
            vmem((128, 512), F32),
            vmem((3, 3, 16, 128), BF16),
            vmem((8, 128), jnp.int32),
            vmem((X * CORES, 8, 128), jnp.int32),
            smem((X * CORES, 8, 128), jnp.int32),
            vmem((GROUPS * Z, 3, 16, 128), BF16),
            vmem((PLANE, 4, 16, 128), BF16),
            vmem((CORES, Y, X, 4, 16, 128), BF16),
            vmem((256, 1024), BF16),
            vmem((16, 16, 512), BF16),
            vmem((512, 256), BF16),
            vmem((3, 128, 512), BF16),
            vmem((3, 128, 512), BF16),
            dma((4,)),
            dma((4,)),
            dma,
            dma((Z, GROUPS)),
            dma((2,)),
            dma((2,)),
            dma((3,)),
            dma((3,)),
        ],
        compiler_params=pltpu.CompilerParams(
            collective_id=0, has_side_effects=True, vmem_limit_bytes=32 * 1024 * 1024
        ),
    )(*(pltpu.with_memory_space_constraint(a, pltpu.HBM) for a in (ancestors, structure, panels, inverse_diag)))


def solution(mesh):
    return jax.shard_map(
        per_device,
        mesh=mesh,
        in_specs=(P("leaf", "rep"), P("leaf", None, None), P("leaf", None), P("leaf", "rep", None)),
        out_specs=(P("leaf", "rep", None), P("leaf", "rep", None)),
        check_vma=False,
    )
```

```python
import jax
import jax.numpy as jnp
from jax import lax
from jax.experimental import pallas as pl
from jax.experimental.pallas import tpu as pltpu
from jax.sharding import PartitionSpec as P

MESH = pl.DeviceIdType.MESH
Z, X, Y, CORES = 16, 4, 4, 2
PLANE = X * Y * CORES
GROUPS = 3
OWNER = (
    tuple((n // 3, n % 3, n % 3 + 1) for n in range(12)),
    ((0, 0, 0), (1, 0, 0), (3, 0, 0), (2, 0, 0), (0, 1, 0), (1, 2, 1), (1, 1, 0), (2, 1, 2), (2, 2, 3), (0, 2, 1), (3, 1, 2), (3, 2, 3)),
    ((0, 0, 2), (0, 1, 3), (3, 0, 0), (1, 0, 2), (1, 1, 3), (2, 0, 0), (2, 1, 1), (3, 1, 1), (1, 2, 0), (2, 2, 0), (3, 2, 0), (0, 2, 0)),
    tuple((n // 3, n % 3, n % 3 + 1) for n in range(12)),
)
SHIFT = ((1, 1, 1, 1), (0, 0, 2, 2), (0, 0, 0, 0))
PLACE = [[None] * 16 for _ in range(3)]
HELD = [[[None] * 3 for _ in range(X)] for _ in range(4)]
for kind in range(4):
    for n, (at_x, entry, steps) in enumerate(OWNER[kind]):
        block, row_group = divmod(12 * kind + n, 16)
        assert block == (3 * kind + entry) // 4 and steps == (3 * kind + entry + SHIFT[block][at_x]) % 4
        assert HELD[kind][at_x][entry] is None and 4 * steps + at_x not in PLACE[block]
        PLACE[block][row_group] = 4 * steps + at_x
        HELD[kind][at_x][entry] = n, steps
JUMPS = (3, -3, 0)
SPREAD = (
    (0, 1), (0, -1), (3, 3), (-3, -3), (1, 1), (-1, -1), (3, 1), (-3, -1), (3, 2), (-3, -2), (6, 1), (-6, -1), (6, 2),
)
STEPS = sorted({step for _, step in SPREAD} | {-step for _, step in SPREAD})
assert sorted({j % Z for j in JUMPS} | {(a + b) % Z for a, b in SPREAD}) == list(range(Z))
assert len(JUMPS) + len(SPREAD) == Z
TARGETS = sorted(
    ((dx, dy, dc) for dx in range(X) for dy in range(Y) for dc in range(CORES)),
    key=lambda d: (-min(d[0], X - d[0]) - min(d[1], Y - d[1]), -d[2], (d[0] + 2 * d[1]) % 4),
)
F32, BF16 = jnp.float32, jnp.bfloat16


def kernel(
    anc_hbm, struct_hbm, panels_hbm, inv_hbm, off, diag,
    struct_ref, anc, panels, inv, pieces, st_send, st_all, st_smem, slots, tiles, stage, picked, lhs, placed, pt,
    d_send, d_recv,
    in_sem, s_sems, spread_send, z_recv, st_sems, pick_sems, d_send_sem, d_recv_sem,
):
    me, y = lax.axis_index("leaf"), lax.axis_index("rep")
    z, x, c = me // 8, (me // 2) % 4, me % 2

    def leaf(zz, xx, cc):
        return (zz * X + xx) * CORES + cc

    def along(step):
        return (z + Z + step) % Z

    def by(index, values):
        return sum(jnp.where(index == n, value, 0) for n, value in enumerate(values))

    shifts = [by(x, values) for values in SHIFT]
    owners = by(8 * (z % 4) + 2 * x + c, [
        sum((1 << 6 * j) * (o[0] + 4 * o[1] + 16 * o[2]) for j, o in enumerate(OWNER[kind][g // 2] for g in range(3 * n, 3 * n + 3)))
        for kind in range(4) for n in range(X * CORES)
    ])

    def sources(from_z):
        return by(4 * (from_z % 4) + x, [
            sum((1 << 6 * e) * (n + 16 * steps) for e, (n, steps) in enumerate(HELD[kind][at])) for kind in range(4) for at in range(X)
        ])

    get_anc = pltpu.make_async_copy(anc_hbm, anc, in_sem.at[3])
    get_panels = pltpu.make_async_copy(panels_hbm.at[0], panels, in_sem.at[0])
    get_inv = pltpu.make_async_copy(inv_hbm.at[0], inv, in_sem.at[1])
    get_struct = pltpu.make_async_copy(struct_hbm, struct_ref, in_sem.at[4])
    get_anc.start()
    get_struct.start()
    get_panels.start()
    get_inv.start()

    barrier = pltpu.get_barrier_semaphore()

    def greet(n, carry):
        there = leaf(z, (x + n // 8) % X, (c + n % 2) % CORES)
        pl.semaphore_signal(barrier, inc=1, device_id=(there, (y + n // 2) % Y), device_id_type=MESH)
        return carry

    for jump in JUMPS:
        if jump:
            held = sources(along(-jump))
            for e in range(GROUPS):
                pair, steps = held // (1 << 6 * e) % 16, held // (1 << 6 * e + 4) % 4
                there = (leaf(along(-jump), pair // 3, (2 * pair + c) // 3 % 2), (y + Y - steps) % Y)
                pl.semaphore_signal(barrier, inc=1, device_id=there, device_id_type=MESH)
    for step in STEPS:
        pl.semaphore_signal(barrier, inc=1, device_id=(leaf(along(step), x, c), y), device_id_type=MESH)
    lax.fori_loop(1, PLANE, greet, 0)

    get_struct.wait()
    lane = lax.broadcasted_iota(jnp.int32, (8, 128), 1)
    blocks = jnp.zeros((8, 128), jnp.int32)
    for q in range(4):
        blocks = jnp.where(lane == q, struct_ref[0, q], blocks)
    slot = 2 * x + c
    st_send[...] = blocks
    st_all[slot] = blocks
    get_anc.wait()
    rows = anc[...].astype(F32)
    for h in range(3):
        for t in range(3):
            halves = [rows[8 * h:8 * h + 8, 256 * t + 128 * k:256 * t + 128 * k + 128] for k in range(2)]
            pieces[h, t] = jnp.concatenate(halves, axis=0).astype(BF16)

    pl.semaphore_wait(barrier, PLANE - 1 + GROUPS * (len(JUMPS) - 1) + len(STEPS))

    def tell(n, carry):
        pltpu.make_async_remote_copy(
            src_ref=st_send, dst_ref=st_all.at[slot], send_sem=st_sems.at[0], recv_sem=st_sems.at[1],
            device_id=(leaf(z, (x + n // 2) % X, (c + n % 2) % CORES), y), device_id_type=MESH,
        ).start()
        return carry

    def owner(j):
        one = owners // (1 << 6 * j) % 64
        return one // 4 % 4, one % 4, (y + one // 16) % Y, (3 * c + j) % 2

    def scatter(j, jump, here):
        entry, to_x, to_y, to_c = owner(j)
        landing = tiles.at[pl.ds(3 * (GROUPS * z + entry), 3)]
        if here:
            return pltpu.make_async_copy(pieces.at[j], landing, z_recv.at[0, entry])
        return pltpu.make_async_remote_copy(
            src_ref=pieces.at[j], dst_ref=landing,
            send_sem=s_sems.at[0] if jump else s_sems.at[1 + j], recv_sem=z_recv.at[jump % Z, entry],
            device_id=(leaf(along(jump), to_x, to_c), to_y), device_id_type=MESH,
        )

    def stays(j):
        _, to_x, to_y, to_c = owner(j)
        return jnp.logical_and(jnp.logical_and(to_x == x, to_y == y), to_c == c)

    for jump in JUMPS:
        for j in range(3):
            if jump:
                scatter(j, jump, False).start()
            else:
                pl.when(stays(j))(lambda: scatter(j, 0, True).start())
                pl.when(jnp.logical_not(stays(j)))(lambda: scatter(j, 0, False).start())
    lax.fori_loop(1, X * CORES, tell, 0)

    landed = set()

    def arrived(o, e):
        if (o, e) not in landed:
            landed.add((o, e))
            pltpu.make_async_copy(pieces.at[0], pieces.at[0], z_recv.at[o % Z, e]).wait()

    def pass_on(o, step, e):
        part = tiles.at[pl.ds(3 * (GROUPS * along(-o) + e), 3)]
        pltpu.make_async_remote_copy(
            src_ref=part, dst_ref=part, send_sem=spread_send, recv_sem=z_recv.at[(o + step) % Z, e],
            device_id=(leaf(along(step), x, c), y), device_id_type=MESH,
        ).start()

    for o, step in SPREAD:
        for e in range(GROUPS):
            if (o + step) % Z == Z // 2:
                arrived(o, e)
                arrived(-o, e)
                pl.when(c == 0)(lambda: pass_on(o, step, e))
                pl.when(c == 1)(lambda: pass_on(-o, -step, e))
            else:
                arrived(o, e)
                pass_on(o, step, e)
    get_panels.wait()
    pt[...] = panels[pl.ds(pl.multiple_of(256 * y, 256), 256), :].T
    told = st_all.at[pl.ds(0, X * CORES - 1)]
    pltpu.make_async_copy(told, told, st_sems.at[1]).wait()
    to_smem = pltpu.make_async_copy(st_all, st_smem, in_sem.at[2])
    to_smem.start()
    def target(n):
        dx, dy, dc = TARGETS[n]
        return (x + dx) % X, (y + dy) % Y, (c + dc) % CORES

    to_smem.wait()
    for n in range(PLANE):
        to_x, to_y, to_c = target(n)
        child = CORES * to_x + to_c
        row = st_smem[child, 0, to_y]
        shift = by(lax.rem(row, 3), shifts)
        for q in range(4):
            column = st_smem[child, 0, q]
            held = 4 * row + lax.rem(y + 8 - shift - lax.div(column, 3), 4)
            slots[n, q] = 3 * held + lax.rem(column, 3)
    for o in range(Z):
        o = o if o < Z // 2 else o - Z
        for e in range(GROUPS):
            arrived(o, e)

    def pick(n):
        for q in range(4):
            stage[n, q] = tiles[slots[n, q]]

    for n in range(PLANE - 1):
        pick(n)
        to_x, to_y, to_c = target(n)
        pltpu.make_async_remote_copy(
            src_ref=stage.at[n], dst_ref=picked.at[c, y, x], send_sem=pick_sems.at[0], recv_sem=pick_sems.at[1],
            device_id=(leaf(z, to_x, to_c), to_y), device_id_type=MESH,
        ).start()
    pick(PLANE - 1)
    pltpu.make_async_copy(stage.at[PLANE - 1], picked.at[c, y, x], pick_sems.at[1]).start()

    pltpu.make_async_copy(picked, picked, pick_sems.at[1]).wait()

    for q in range(4):
        quarter = lax.div(struct_ref[0, q], 3)
        for part in range(4):
            pair = [picked[k, lax.rem(quarter + part, 4), :, q].astype(F32).reshape(X, 2, 8, 128) for k in range(CORES)]
            for k in range(2):
                rows64 = jnp.concatenate([pair[0][:, k], pair[1][:, k]], axis=1).astype(BF16).reshape(64, 128)
                lhs[64 * part:64 * part + 64, 256 * q + 128 * k:256 * q + 128 * k + 128] = rows64
    update = (-jnp.dot(lhs[...], panels[...], preferred_element_type=F32)).astype(BF16)
    placed[...] = update.reshape(16, 16, 512)
    kind = lax.rem(by(y, [struct_ref[0, q] for q in range(4)]), 3)
    for first in range(0, 16, 4):
        places = by(kind, [sum(PLACE[n][first + m] << 4 * m for m in range(4)) for n in range(3)])
        for m in range(4):
            off[0, 16 * (first + m):16 * (first + m) + 16] = placed[lax.rem(lax.div(places, 1 << 4 * m), 16)]

    def share(r):
        return jnp.dot(pt[pl.ds(pl.multiple_of(128 * r, 128), 128), :], off[0], preferred_element_type=F32)

    def give(j):
        return pltpu.make_async_remote_copy(
            src_ref=d_send.at[j], dst_ref=d_recv.at[j], send_sem=d_send_sem.at[j], recv_sem=d_recv_sem.at[j],
            device_id=(me, (y + j + 1) % Y), device_id_type=MESH,
        )

    for j in (1, 0, 2):
        d_send[j] = share((y + j + 1) % Y).astype(BF16)
        give(j).start()
    get_inv.wait()
    diag[0] = inv[...] - share(y)
    for j in (0, 2, 1):
        give(j).wait_recv()
        diag[0] -= d_recv[j].astype(F32)

    pltpu.make_async_copy(told, told, st_sems.at[0]).wait()
    for j in range(3):
        pl.when(jnp.logical_not(stays(j)))(lambda: scatter(j, 0, False).wait_send())
    jumped = tiles.at[pl.ds(0, 3 * GROUPS * (len(JUMPS) - 1))]
    pltpu.make_async_copy(jumped, jumped, s_sems.at[0]).wait()
    passed = tiles.at[pl.ds(0, 3 * GROUPS * len(SPREAD))]
    pltpu.make_async_copy(passed, passed, spread_send).wait()
    sent = stage.at[pl.ds(0, PLANE - 1)]
    pltpu.make_async_copy(sent, sent, pick_sems.at[0]).wait()
    for j in range(3):
        give(j).wait_send()


def per_device(ancestors, panels, structure, inverse_diag):
    vmem, smem, dma = pltpu.VMEM, pltpu.SMEM, pltpu.SemaphoreType.DMA
    return pl.pallas_call(
        kernel,
        out_shape=(
            pltpu.VMEM((1, 256, 512), BF16),
            pltpu.VMEM((1, 128, 512), F32),
        ),
        in_specs=[
            pl.BlockSpec(memory_space=pl.ANY),
            pl.BlockSpec(memory_space=pl.ANY),
            pl.BlockSpec(memory_space=pl.ANY),
            pl.BlockSpec(memory_space=pl.ANY),
        ],
        out_specs=(pl.BlockSpec(memory_space=vmem), pl.BlockSpec(memory_space=vmem)),
        scratch_shapes=[
            smem((1, 4), jnp.int32),
            vmem((24, 768), BF16),
            vmem((1024, 512), BF16),
            vmem((128, 512), F32),
            vmem((3, 3, 16, 128), BF16),
            vmem((8, 128), jnp.int32),
            vmem((X * CORES, 8, 128), jnp.int32),
            smem((X * CORES, 8, 128), jnp.int32),
            smem((PLANE, 4), jnp.int32),
            vmem((GROUPS * Z * 3, 16, 128), BF16),
            vmem((PLANE, 4, 16, 128), BF16),
            vmem((CORES, Y, X, 4, 16, 128), BF16),
            vmem((256, 1024), BF16),
            vmem((16, 16, 512), BF16),
            vmem((512, 256), BF16),
            vmem((3, 128, 512), BF16),
            vmem((3, 128, 512), BF16),
            dma((5,)),
            dma((4,)),
            dma,
            dma((Z, GROUPS)),
            dma((2,)),
            dma((2,)),
            dma((3,)),
            dma((3,)),
        ],
        compiler_params=pltpu.CompilerParams(
            collective_id=0, has_side_effects=True, vmem_limit_bytes=32 * 1024 * 1024
        ),
    )(*(pltpu.with_memory_space_constraint(a, pltpu.HBM) for a in (ancestors, structure, panels, inverse_diag)))


def solution(mesh):
    return jax.shard_map(
        per_device,
        mesh=mesh,
        in_specs=(P("leaf", "rep"), P("leaf", None, None), P("leaf", None), P("leaf", "rep", None)),
        out_specs=(P("leaf", "rep", None), P("leaf", "rep", None)),
        check_vma=False,
    )
```

```python
import jax
import jax.numpy as jnp
from jax import lax
from jax.experimental import pallas as pl
from jax.experimental.pallas import tpu as pltpu
from jax.sharding import PartitionSpec as P

MESH = pl.DeviceIdType.MESH
Z, X, Y, CORES = 16, 4, 4, 2
PLANE = X * Y * CORES
GROUPS = 3
OWNER = (
    tuple((n // 3, n % 3, n % 3 + 1) for n in range(12)),
    ((0, 0, 0), (1, 0, 0), (3, 0, 0), (2, 0, 0), (0, 1, 0), (1, 2, 1), (1, 1, 0), (2, 1, 2), (2, 2, 3), (0, 2, 1), (3, 1, 2), (3, 2, 3)),
    ((0, 0, 2), (0, 1, 3), (3, 0, 0), (1, 0, 2), (1, 1, 3), (2, 0, 0), (2, 1, 1), (3, 1, 1), (1, 2, 0), (2, 2, 0), (3, 2, 0), (0, 2, 0)),
    tuple((n // 3, n % 3, n % 3 + 1) for n in range(12)),
)
SHIFT = ((1, 1, 1, 1), (0, 0, 2, 2), (0, 0, 0, 0))
PLACE = [[None] * 16 for _ in range(3)]
HELD = [[[None] * 3 for _ in range(X)] for _ in range(4)]
for kind in range(4):
    for n, (at_x, entry, steps) in enumerate(OWNER[kind]):
        block, row_group = divmod(12 * kind + n, 16)
        assert block == (3 * kind + entry) // 4 and steps == (3 * kind + entry + SHIFT[block][at_x]) % 4
        assert HELD[kind][at_x][entry] is None and 4 * steps + at_x not in PLACE[block]
        PLACE[block][row_group] = 4 * steps + at_x
        HELD[kind][at_x][entry] = n, steps
JUMPS = (3, -3, 0)
SPREAD = (
    (0, 1), (0, -1), (3, 3), (-3, -3), (1, 1), (-1, -1), (3, 1), (-3, -1), (3, 2), (-3, -2), (6, 1), (-6, -1), (6, 2),
)
STEPS = sorted({step for _, step in SPREAD} | {-step for _, step in SPREAD})
assert sorted({j % Z for j in JUMPS} | {(a + b) % Z for a, b in SPREAD}) == list(range(Z))
assert len(JUMPS) + len(SPREAD) == Z
TARGETS = sorted(
    ((dx, dy, dc) for dx in range(X) for dy in range(Y) for dc in range(CORES)),
    key=lambda d: (d == (0, 0, 0), -d[2], -min(d[0], X - d[0]) - min(d[1], Y - d[1])),
)
F32, BF16 = jnp.float32, jnp.bfloat16


def kernel(
    anc_hbm, struct_hbm, panels_hbm, inv_hbm, off, diag,
    struct_ref, anc, panels, inv, pieces, st_send, st_all, st_smem, slots, tiles, stage, picked, lhs, placed, pt,
    d_send, d_recv,
    in_sem, s_sems, spread_send, z_recv, st_sems, pick_sems, d_send_sem, d_recv_sem,
):
    me, y = lax.axis_index("leaf"), lax.axis_index("rep")
    z, x, c = me // 8, (me // 2) % 4, me % 2

    def leaf(zz, xx, cc):
        return (zz * X + xx) * CORES + cc

    def along(step):
        return (z + Z + step) % Z

    def by(index, values):
        return sum(jnp.where(index == n, value, 0) for n, value in enumerate(values))

    shifts = [by(x, values) for values in SHIFT]
    owners = by(8 * (z % 4) + 2 * x + c, [
        sum((1 << 6 * j) * (o[0] + 4 * o[1] + 16 * o[2]) for j, o in enumerate(OWNER[kind][g // 2] for g in range(3 * n, 3 * n + 3)))
        for kind in range(4) for n in range(X * CORES)
    ])

    def sources(from_z):
        return by(4 * (from_z % 4) + x, [
            sum((1 << 6 * e) * (n + 16 * steps) for e, (n, steps) in enumerate(HELD[kind][at])) for kind in range(4) for at in range(X)
        ])

    get_anc = pltpu.make_async_copy(anc_hbm, anc, in_sem.at[3])
    get_panels = pltpu.make_async_copy(panels_hbm.at[0], panels, in_sem.at[0])
    get_inv = pltpu.make_async_copy(inv_hbm.at[0], inv, in_sem.at[1])
    get_struct = pltpu.make_async_copy(struct_hbm, struct_ref, in_sem.at[4])
    get_anc.start()
    get_struct.start()
    get_panels.start()
    get_inv.start()

    barrier = pltpu.get_barrier_semaphore()

    def greet(n, carry):
        there = leaf(z, (x + n // 8) % X, (c + n % 2) % CORES)
        pl.semaphore_signal(barrier, inc=1, device_id=(there, (y + n // 2) % Y), device_id_type=MESH)
        return carry

    for jump in JUMPS:
        if jump:
            held = sources(along(-jump))
            for e in range(GROUPS):
                pair, steps = held // (1 << 6 * e) % 16, held // (1 << 6 * e + 4) % 4
                there = (leaf(along(-jump), pair // 3, (2 * pair + c) // 3 % 2), (y + Y - steps) % Y)
                pl.semaphore_signal(barrier, inc=1, device_id=there, device_id_type=MESH)
    for step in STEPS:
        pl.semaphore_signal(barrier, inc=1, device_id=(leaf(along(step), x, c), y), device_id_type=MESH)
    lax.fori_loop(1, PLANE, greet, 0)

    get_struct.wait()
    lane = lax.broadcasted_iota(jnp.int32, (8, 128), 1)
    blocks = jnp.zeros((8, 128), jnp.int32)
    for q in range(4):
        blocks = jnp.where(lane == q, struct_ref[0, q], blocks)
    slot = 2 * x + c
    st_send[...] = blocks
    st_all[slot] = blocks
    get_anc.wait()
    rows = anc[...].astype(F32)
    for h in range(3):
        for t in range(3):
            halves = [rows[8 * h:8 * h + 8, 256 * t + 128 * k:256 * t + 128 * k + 128] for k in range(2)]
            pieces[h, t] = jnp.concatenate(halves, axis=0).astype(BF16)

    pl.semaphore_wait(barrier, PLANE - 1 + GROUPS * (len(JUMPS) - 1) + len(STEPS))

    def tell(n, carry):
        pltpu.make_async_remote_copy(
            src_ref=st_send, dst_ref=st_all.at[slot], send_sem=st_sems.at[0], recv_sem=st_sems.at[1],
            device_id=(leaf(z, (x + n // 2) % X, (c + n % 2) % CORES), y), device_id_type=MESH,
        ).start()
        return carry

    def owner(j):
        one = owners // (1 << 6 * j) % 64
        return one // 4 % 4, one % 4, (y + one // 16) % Y, (3 * c + j) % 2

    def scatter(j, jump, here):
        entry, to_x, to_y, to_c = owner(j)
        landing = tiles.at[pl.ds(3 * (GROUPS * z + entry), 3)]
        if here:
            return pltpu.make_async_copy(pieces.at[j], landing, z_recv.at[0, entry])
        return pltpu.make_async_remote_copy(
            src_ref=pieces.at[j], dst_ref=landing,
            send_sem=s_sems.at[0] if jump else s_sems.at[1 + j], recv_sem=z_recv.at[jump % Z, entry],
            device_id=(leaf(along(jump), to_x, to_c), to_y), device_id_type=MESH,
        )

    def stays(j):
        _, to_x, to_y, to_c = owner(j)
        return jnp.logical_and(jnp.logical_and(to_x == x, to_y == y), to_c == c)

    for jump in JUMPS:
        for j in range(3):
            if jump:
                scatter(j, jump, False).start()
            else:
                pl.when(stays(j))(lambda: scatter(j, 0, True).start())
                pl.when(jnp.logical_not(stays(j)))(lambda: scatter(j, 0, False).start())
    lax.fori_loop(1, X * CORES, tell, 0)

    landed = set()

    def arrived(o, e):
        if (o, e) not in landed:
            landed.add((o, e))
            pltpu.make_async_copy(pieces.at[0], pieces.at[0], z_recv.at[o % Z, e]).wait()

    def pass_on(o, step, e):
        part = tiles.at[pl.ds(3 * (GROUPS * along(-o) + e), 3)]
        pltpu.make_async_remote_copy(
            src_ref=part, dst_ref=part, send_sem=spread_send, recv_sem=z_recv.at[(o + step) % Z, e],
            device_id=(leaf(along(step), x, c), y), device_id_type=MESH,
        ).start()

    for o, step in SPREAD:
        for e in range(GROUPS):
            if (o + step) % Z == Z // 2:
                arrived(o, e)
                arrived(-o, e)
                pl.when(c == 0)(lambda: pass_on(o, step, e))
                pl.when(c == 1)(lambda: pass_on(-o, -step, e))
            else:
                arrived(o, e)
                pass_on(o, step, e)
    get_panels.wait()
    pt[...] = panels[pl.ds(pl.multiple_of(256 * y, 256), 256), :].T
    told = st_all.at[pl.ds(0, X * CORES - 1)]
    pltpu.make_async_copy(told, told, st_sems.at[1]).wait()
    to_smem = pltpu.make_async_copy(st_all, st_smem, in_sem.at[2])
    to_smem.start()
    def target(n):
        dx, dy, dc = TARGETS[n]
        return (x + dx) % X, (y + dy) % Y, (c + dc) % CORES

    to_smem.wait()
    for n in range(PLANE):
        to_x, to_y, to_c = target(n)
        child = CORES * to_x + to_c
        row = st_smem[child, 0, to_y]
        shift = by(lax.rem(row, 3), shifts)
        for q in range(4):
            column = st_smem[child, 0, q]
            held = 4 * row + lax.rem(y + 8 - shift - lax.div(column, 3), 4)
            slots[n, q] = 3 * held + lax.rem(column, 3)
    for o in range(Z):
        o = o if o < Z // 2 else o - Z
        for e in range(GROUPS):
            arrived(o, e)

    def pick(n):
        for q in range(4):
            stage[n, q] = tiles[slots[n, q]]

    for n in range(PLANE - 1):
        pick(n)
        to_x, to_y, to_c = target(n)
        pltpu.make_async_remote_copy(
            src_ref=stage.at[n], dst_ref=picked.at[c, y, x], send_sem=pick_sems.at[0], recv_sem=pick_sems.at[1],
            device_id=(leaf(z, to_x, to_c), to_y), device_id_type=MESH,
        ).start()
    pick(PLANE - 1)
    pltpu.make_async_copy(stage.at[PLANE - 1], picked.at[c, y, x], pick_sems.at[1]).start()

    pltpu.make_async_copy(picked, picked, pick_sems.at[1]).wait()

    for q in range(4):
        quarter = lax.div(struct_ref[0, q], 3)
        for part in range(4):
            pair = [picked[k, lax.rem(quarter + part, 4), :, q].astype(F32).reshape(X, 2, 8, 128) for k in range(CORES)]
            for k in range(2):
                rows64 = jnp.concatenate([pair[0][:, k], pair[1][:, k]], axis=1).astype(BF16).reshape(64, 128)
                lhs[64 * part:64 * part + 64, 256 * q + 128 * k:256 * q + 128 * k + 128] = rows64
    update = (-jnp.dot(lhs[...], panels[...], preferred_element_type=F32)).astype(BF16)
    placed[...] = update.reshape(16, 16, 512)
    kind = lax.rem(by(y, [struct_ref[0, q] for q in range(4)]), 3)
    for first in range(0, 16, 4):
        places = by(kind, [sum(PLACE[n][first + m] << 4 * m for m in range(4)) for n in range(3)])
        for m in range(4):
            off[0, 16 * (first + m):16 * (first + m) + 16] = placed[lax.rem(lax.div(places, 1 << 4 * m), 16)]

    def share(r):
        return jnp.dot(pt[pl.ds(pl.multiple_of(128 * r, 128), 128), :], off[0], preferred_element_type=F32)

    def give(j):
        return pltpu.make_async_remote_copy(
            src_ref=d_send.at[j], dst_ref=d_recv.at[j], send_sem=d_send_sem.at[j], recv_sem=d_recv_sem.at[j],
            device_id=(me, (y + j + 1) % Y), device_id_type=MESH,
        )

    for j in (0, 2, 1):
        d_send[j] = share((y + j + 1) % Y).astype(BF16)
        give(j).start()
    get_inv.wait()
    diag[0] = inv[...] - share(y)
    for j in (0, 2, 1):
        give(j).wait_recv()
        diag[0] -= d_recv[j].astype(F32)

    pltpu.make_async_copy(told, told, st_sems.at[0]).wait()
    for j in range(3):
        pl.when(jnp.logical_not(stays(j)))(lambda: scatter(j, 0, False).wait_send())
    jumped = tiles.at[pl.ds(0, 3 * GROUPS * (len(JUMPS) - 1))]
    pltpu.make_async_copy(jumped, jumped, s_sems.at[0]).wait()
    passed = tiles.at[pl.ds(0, 3 * GROUPS * len(SPREAD))]
    pltpu.make_async_copy(passed, passed, spread_send).wait()
    sent = stage.at[pl.ds(0, PLANE - 1)]
    pltpu.make_async_copy(sent, sent, pick_sems.at[0]).wait()
    for j in range(3):
        give(j).wait_send()


def write_out(off, diag, off_hbm, diag_hbm, sems):
    put = [pltpu.make_async_copy(*pair) for pair in ((off, off_hbm, sems.at[0]), (diag, diag_hbm, sems.at[1]))]
    for copy in put:
        copy.start()
    for copy in put:
        copy.wait()


def per_device(ancestors, panels, structure, inverse_diag):
    vmem, smem, dma = pltpu.VMEM, pltpu.SMEM, pltpu.SemaphoreType.DMA
    results = pl.pallas_call(
        kernel,
        out_shape=(
            pltpu.VMEM((1, 256, 512), BF16),
            pltpu.VMEM((1, 128, 512), F32),
        ),
        in_specs=[
            pl.BlockSpec(memory_space=pl.ANY),
            pl.BlockSpec(memory_space=pl.ANY),
            pl.BlockSpec(memory_space=pl.ANY),
            pl.BlockSpec(memory_space=pl.ANY),
        ],
        out_specs=(pl.BlockSpec(memory_space=vmem), pl.BlockSpec(memory_space=vmem)),
        scratch_shapes=[
            smem((1, 4), jnp.int32),
            vmem((24, 768), BF16),
            vmem((1024, 512), BF16),
            vmem((128, 512), F32),
            vmem((3, 3, 16, 128), BF16),
            vmem((8, 128), jnp.int32),
            vmem((X * CORES, 8, 128), jnp.int32),
            smem((X * CORES, 8, 128), jnp.int32),
            smem((PLANE, 4), jnp.int32),
            vmem((GROUPS * Z * 3, 16, 128), BF16),
            vmem((PLANE, 4, 16, 128), BF16),
            vmem((CORES, Y, X, 4, 16, 128), BF16),
            vmem((256, 1024), BF16),
            vmem((16, 16, 512), BF16),
            vmem((512, 256), BF16),
            vmem((3, 128, 512), BF16),
            vmem((3, 128, 512), BF16),
            dma((5,)),
            dma((4,)),
            dma,
            dma((Z, GROUPS)),
            dma((2,)),
            dma((2,)),
            dma((3,)),
            dma((3,)),
        ],
        compiler_params=pltpu.CompilerParams(
            collective_id=0, has_side_effects=True, vmem_limit_bytes=32 * 1024 * 1024
        ),
    )(*(pltpu.with_memory_space_constraint(a, pltpu.HBM) for a in (ancestors, structure, panels, inverse_diag)))
    return pl.pallas_call(
        write_out,
        out_shape=(pltpu.HBM((1, 256, 512), BF16), pltpu.HBM((1, 128, 512), F32)),
        in_specs=[pl.BlockSpec(memory_space=vmem)] * 2,
        out_specs=(pl.BlockSpec(memory_space=pl.ANY),) * 2,
        scratch_shapes=[dma((2,))],
    )(*(pltpu.with_memory_space_constraint(a, pltpu.VMEM) for a in results))


def solution(mesh):
    return jax.shard_map(
        per_device,
        mesh=mesh,
        in_specs=(P("leaf", "rep"), P("leaf", None, None), P("leaf", None), P("leaf", "rep", None)),
        out_specs=(P("leaf", "rep", None), P("leaf", "rep", None)),
        check_vma=False,
    )
```

```python
import jax
import jax.numpy as jnp
from jax import lax
from jax.experimental import pallas as pl
from jax.experimental.pallas import tpu as pltpu
from jax.sharding import PartitionSpec as P

MESH = pl.DeviceIdType.MESH
Z, X, Y, CORES = 16, 4, 4, 2
PLANE = X * Y * CORES
GROUPS = 3
OWNER = (
    tuple((n // 3, n % 3, n % 3 + 1) for n in range(12)),
    ((0, 0, 0), (1, 0, 0), (3, 0, 0), (2, 0, 0), (0, 1, 0), (1, 2, 1), (1, 1, 0), (2, 1, 2), (2, 2, 3), (0, 2, 1), (3, 1, 2), (3, 2, 3)),
    ((0, 0, 2), (0, 1, 3), (3, 0, 0), (1, 0, 2), (1, 1, 3), (2, 0, 0), (2, 1, 1), (3, 1, 1), (1, 2, 0), (2, 2, 0), (3, 2, 0), (0, 2, 0)),
    tuple((n // 3, n % 3, n % 3 + 1) for n in range(12)),
)
SHIFT = ((1, 1, 1, 1), (0, 0, 2, 2), (0, 0, 0, 0))
PLACE = [[None] * 16 for _ in range(3)]
HELD = [[[None] * 3 for _ in range(X)] for _ in range(4)]
for kind in range(4):
    for n, (at_x, entry, steps) in enumerate(OWNER[kind]):
        block, row_group = divmod(12 * kind + n, 16)
        assert block == (3 * kind + entry) // 4 and steps == (3 * kind + entry + SHIFT[block][at_x]) % 4
        assert HELD[kind][at_x][entry] is None and 4 * steps + at_x not in PLACE[block]
        PLACE[block][row_group] = 4 * steps + at_x
        HELD[kind][at_x][entry] = n, steps
JUMPS = (3, -3, 0)
SPREAD = (
    (0, 1), (0, -1), (3, 3), (-3, -3), (1, 1), (-1, -1), (3, 1), (-3, -1), (3, 2), (-3, -2), (6, 1), (-6, -1), (6, 2),
)
STEPS = sorted({step for _, step in SPREAD} | {-step for _, step in SPREAD})
assert sorted({j % Z for j in JUMPS} | {(a + b) % Z for a, b in SPREAD}) == list(range(Z))
assert len(JUMPS) + len(SPREAD) == Z
TARGETS = sorted(
    ((dx, dy, dc) for dx in range(X) for dy in range(Y) for dc in range(CORES)),
    key=lambda d: (d == (0, 0, 0), -d[2], -min(d[0], X - d[0]) - min(d[1], Y - d[1])),
)
F32, BF16 = jnp.float32, jnp.bfloat16


def kernel(
    anc_hbm, struct_hbm, panels_hbm, inv_hbm, off, diag,
    struct_ref, anc, panels, inv, pieces, st_send, st_all, st_smem, slots, tiles, stage, picked, lhs, placed, pt,
    d_send, d_recv,
    in_sem, s_sems, spread_send, z_recv, st_sems, pick_sems, d_send_sem, d_recv_sem,
):
    me, y = lax.axis_index("leaf"), lax.axis_index("rep")
    z, x, c = me // 8, (me // 2) % 4, me % 2

    def leaf(zz, xx, cc):
        return (zz * X + xx) * CORES + cc

    def along(step):
        return (z + Z + step) % Z

    def by(index, values):
        return sum(jnp.where(index == n, value, 0) for n, value in enumerate(values))

    shifts = [by(x, values) for values in SHIFT]
    owners = by(8 * (z % 4) + 2 * x + c, [
        sum((1 << 6 * j) * (o[0] + 4 * o[1] + 16 * o[2]) for j, o in enumerate(OWNER[kind][g // 2] for g in range(3 * n, 3 * n + 3)))
        for kind in range(4) for n in range(X * CORES)
    ])

    def sources(from_z):
        return by(4 * (from_z % 4) + x, [
            sum((1 << 6 * e) * (n + 16 * steps) for e, (n, steps) in enumerate(HELD[kind][at])) for kind in range(4) for at in range(X)
        ])

    get_anc = pltpu.make_async_copy(anc_hbm, anc, in_sem.at[3])
    get_panels = pltpu.make_async_copy(panels_hbm.at[0], panels, in_sem.at[0])
    get_inv = pltpu.make_async_copy(inv_hbm.at[0], inv, in_sem.at[1])
    get_struct = pltpu.make_async_copy(struct_hbm, struct_ref, in_sem.at[4])
    get_anc.start()
    get_struct.start()
    get_panels.start()
    get_inv.start()

    barrier = pltpu.get_barrier_semaphore()

    def greet(n, carry):
        there = leaf(z, (x + n // 8) % X, (c + n % 2) % CORES)
        pl.semaphore_signal(barrier, inc=1, device_id=(there, (y + n // 2) % Y), device_id_type=MESH)
        return carry

    for jump in JUMPS:
        if jump:
            held = sources(along(-jump))
            for e in range(GROUPS):
                pair, steps = held // (1 << 6 * e) % 16, held // (1 << 6 * e + 4) % 4
                there = (leaf(along(-jump), pair // 3, (2 * pair + c) // 3 % 2), (y + Y - steps) % Y)
                pl.semaphore_signal(barrier, inc=1, device_id=there, device_id_type=MESH)
    for step in STEPS:
        pl.semaphore_signal(barrier, inc=1, device_id=(leaf(along(step), x, c), y), device_id_type=MESH)
    lax.fori_loop(1, PLANE, greet, 0)

    get_struct.wait()
    lane = lax.broadcasted_iota(jnp.int32, (8, 128), 1)
    blocks = jnp.zeros((8, 128), jnp.int32)
    for q in range(4):
        blocks = jnp.where(lane == q, struct_ref[0, q], blocks)
    slot = 2 * x + c
    st_send[...] = blocks
    st_all[slot] = blocks
    get_anc.wait()
    rows = anc[...].astype(F32)
    for h in range(3):
        for t in range(3):
            halves = [rows[8 * h:8 * h + 8, 256 * t + 128 * k:256 * t + 128 * k + 128] for k in range(2)]
            pieces[h, t] = jnp.concatenate(halves, axis=0).astype(BF16)

    pl.semaphore_wait(barrier, PLANE - 1 + GROUPS * (len(JUMPS) - 1) + len(STEPS))

    def tell(n, carry):
        pltpu.make_async_remote_copy(
            src_ref=st_send, dst_ref=st_all.at[slot], send_sem=st_sems.at[0], recv_sem=st_sems.at[1],
            device_id=(leaf(z, (x + n // 2) % X, (c + n % 2) % CORES), y), device_id_type=MESH,
        ).start()
        return carry

    def owner(j):
        one = owners // (1 << 6 * j) % 64
        return one // 4 % 4, one % 4, (y + one // 16) % Y, (3 * c + j) % 2

    def scatter(j, jump, here):
        entry, to_x, to_y, to_c = owner(j)
        landing = tiles.at[pl.ds(3 * (GROUPS * z + entry), 3)]
        if here:
            return pltpu.make_async_copy(pieces.at[j], landing, z_recv.at[0, entry])
        return pltpu.make_async_remote_copy(
            src_ref=pieces.at[j], dst_ref=landing,
            send_sem=s_sems.at[0] if jump else s_sems.at[1 + j], recv_sem=z_recv.at[jump % Z, entry],
            device_id=(leaf(along(jump), to_x, to_c), to_y), device_id_type=MESH,
        )

    def stays(j):
        _, to_x, to_y, to_c = owner(j)
        return jnp.logical_and(jnp.logical_and(to_x == x, to_y == y), to_c == c)

    for jump in JUMPS:
        for j in range(3):
            if jump:
                scatter(j, jump, False).start()
            else:
                pl.when(stays(j))(lambda: scatter(j, 0, True).start())
                pl.when(jnp.logical_not(stays(j)))(lambda: scatter(j, 0, False).start())
    lax.fori_loop(1, X * CORES, tell, 0)

    landed = set()

    def arrived(o, e):
        if (o, e) not in landed:
            landed.add((o, e))
            pltpu.make_async_copy(pieces.at[0], pieces.at[0], z_recv.at[o % Z, e]).wait()

    def pass_on(o, step, e):
        part = tiles.at[pl.ds(3 * (GROUPS * along(-o) + e), 3)]
        pltpu.make_async_remote_copy(
            src_ref=part, dst_ref=part, send_sem=spread_send, recv_sem=z_recv.at[(o + step) % Z, e],
            device_id=(leaf(along(step), x, c), y), device_id_type=MESH,
        ).start()

    for o, step in SPREAD:
        for e in range(GROUPS):
            if (o + step) % Z == Z // 2:
                arrived(o, e)
                arrived(-o, e)
                pl.when(c == 0)(lambda: pass_on(o, step, e))
                pl.when(c == 1)(lambda: pass_on(-o, -step, e))
            else:
                arrived(o, e)
                pass_on(o, step, e)
    get_panels.wait()
    pt[...] = panels[pl.ds(pl.multiple_of(256 * y, 256), 256), :].T
    told = st_all.at[pl.ds(0, X * CORES - 1)]
    pltpu.make_async_copy(told, told, st_sems.at[1]).wait()
    to_smem = pltpu.make_async_copy(st_all, st_smem, in_sem.at[2])
    to_smem.start()
    def target(n):
        dx, dy, dc = TARGETS[n]
        return (x + dx) % X, (y + dy) % Y, (c + dc) % CORES

    to_smem.wait()
    for n in range(PLANE):
        to_x, to_y, to_c = target(n)
        child = CORES * to_x + to_c
        row = st_smem[child, 0, to_y]
        shift = by(lax.rem(row, 3), shifts)
        for q in range(4):
            column = st_smem[child, 0, q]
            held = 4 * row + lax.rem(y + 8 - shift - lax.div(column, 3), 4)
            slots[n, q] = 3 * held + lax.rem(column, 3)
    for o in range(Z):
        o = o if o < Z // 2 else o - Z
        for e in range(GROUPS):
            arrived(o, e)

    def pick(n):
        for q in range(4):
            stage[n, q] = tiles[slots[n, q]]

    for n in range(PLANE - 1):
        pick(n)
        to_x, to_y, to_c = target(n)
        pltpu.make_async_remote_copy(
            src_ref=stage.at[n], dst_ref=picked.at[c, y, x], send_sem=pick_sems.at[0], recv_sem=pick_sems.at[1],
            device_id=(leaf(z, to_x, to_c), to_y), device_id_type=MESH,
        ).start()
    pick(PLANE - 1)
    pltpu.make_async_copy(stage.at[PLANE - 1], picked.at[c, y, x], pick_sems.at[1]).start()

    pltpu.make_async_copy(picked, picked, pick_sems.at[1]).wait()

    for q in range(4):
        quarter = lax.div(struct_ref[0, q], 3)
        for part in range(4):
            pair = [picked[k, lax.rem(quarter + part, 4), :, q].astype(F32).reshape(X, 2, 8, 128) for k in range(CORES)]
            for k in range(2):
                rows64 = jnp.concatenate([pair[0][:, k], pair[1][:, k]], axis=1).astype(BF16).reshape(64, 128)
                lhs[64 * part:64 * part + 64, 256 * q + 128 * k:256 * q + 128 * k + 128] = rows64
    update = (-jnp.dot(lhs[...], panels[...], preferred_element_type=F32)).astype(BF16)
    placed[...] = update.reshape(16, 16, 512)
    kind = lax.rem(by(y, [struct_ref[0, q] for q in range(4)]), 3)
    for first in range(0, 16, 4):
        places = by(kind, [sum(PLACE[n][first + m] << 4 * m for m in range(4)) for n in range(3)])
        for m in range(4):
            off[0, 16 * (first + m):16 * (first + m) + 16] = placed[lax.rem(lax.div(places, 1 << 4 * m), 16)]

    def share(row, count):
        return jnp.dot(pt[pl.ds(pl.multiple_of(row, count), count), :], off[0], preferred_element_type=F32)

    def give(j, half):
        rows = pl.ds(64 * half, 64)
        return pltpu.make_async_remote_copy(
            src_ref=d_send.at[j, rows], dst_ref=d_recv.at[j, rows],
            send_sem=d_send_sem.at[j, half], recv_sem=d_recv_sem.at[j, half],
            device_id=(me, (y + j + 1) % Y), device_id_type=MESH,
        )

    for half in range(2):
        for j in (1, 0, 2):
            row = 128 * ((y + j + 1) % Y) + 64 * half
            d_send[j, 64 * half:64 * half + 64] = share(row, 64).astype(BF16)
            give(j, half).start()
    get_inv.wait()
    diag[0] = inv[...] - share(128 * y, 128)
    for j in (0, 2, 1):
        for half in range(2):
            give(j, half).wait_recv()
        diag[0] -= d_recv[j].astype(F32)

    pltpu.make_async_copy(told, told, st_sems.at[0]).wait()
    for j in range(3):
        pl.when(jnp.logical_not(stays(j)))(lambda: scatter(j, 0, False).wait_send())
    jumped = tiles.at[pl.ds(0, 3 * GROUPS * (len(JUMPS) - 1))]
    pltpu.make_async_copy(jumped, jumped, s_sems.at[0]).wait()
    passed = tiles.at[pl.ds(0, 3 * GROUPS * len(SPREAD))]
    pltpu.make_async_copy(passed, passed, spread_send).wait()
    sent = stage.at[pl.ds(0, PLANE - 1)]
    pltpu.make_async_copy(sent, sent, pick_sems.at[0]).wait()
    for j in range(3):
        for half in range(2):
            give(j, half).wait_send()


def write_out(off, diag, off_hbm, diag_hbm, sems):
    put = [pltpu.make_async_copy(*pair) for pair in ((off, off_hbm, sems.at[0]), (diag, diag_hbm, sems.at[1]))]
    for copy in put:
        copy.start()
    for copy in put:
        copy.wait()


def per_device(ancestors, panels, structure, inverse_diag):
    vmem, smem, dma = pltpu.VMEM, pltpu.SMEM, pltpu.SemaphoreType.DMA
    results = pl.pallas_call(
        kernel,
        out_shape=(
            pltpu.VMEM((1, 256, 512), BF16),
            pltpu.VMEM((1, 128, 512), F32),
        ),
        in_specs=[
            pl.BlockSpec(memory_space=pl.ANY),
            pl.BlockSpec(memory_space=pl.ANY),
            pl.BlockSpec(memory_space=pl.ANY),
            pl.BlockSpec(memory_space=pl.ANY),
        ],
        out_specs=(pl.BlockSpec(memory_space=vmem), pl.BlockSpec(memory_space=vmem)),
        scratch_shapes=[
            smem((1, 4), jnp.int32),
            vmem((24, 768), BF16),
            vmem((1024, 512), BF16),
            vmem((128, 512), F32),
            vmem((3, 3, 16, 128), BF16),
            vmem((8, 128), jnp.int32),
            vmem((X * CORES, 8, 128), jnp.int32),
            smem((X * CORES, 8, 128), jnp.int32),
            smem((PLANE, 4), jnp.int32),
            vmem((GROUPS * Z * 3, 16, 128), BF16),
            vmem((PLANE, 4, 16, 128), BF16),
            vmem((CORES, Y, X, 4, 16, 128), BF16),
            vmem((256, 1024), BF16),
            vmem((16, 16, 512), BF16),
            vmem((512, 256), BF16),
            vmem((3, 128, 512), BF16),
            vmem((3, 128, 512), BF16),
            dma((5,)),
            dma((4,)),
            dma,
            dma((Z, GROUPS)),
            dma((2,)),
            dma((2,)),
            dma((3, 2)),
            dma((3, 2)),
        ],
        compiler_params=pltpu.CompilerParams(
            collective_id=0, has_side_effects=True, vmem_limit_bytes=32 * 1024 * 1024
        ),
    )(*(pltpu.with_memory_space_constraint(a, pltpu.HBM) for a in (ancestors, structure, panels, inverse_diag)))
    return pl.pallas_call(
        write_out,
        out_shape=(pltpu.HBM((1, 256, 512), BF16), pltpu.HBM((1, 128, 512), F32)),
        in_specs=[pl.BlockSpec(memory_space=vmem)] * 2,
        out_specs=(pl.BlockSpec(memory_space=pl.ANY),) * 2,
        scratch_shapes=[dma((2,))],
    )(*(pltpu.with_memory_space_constraint(a, pltpu.VMEM) for a in results))


def solution(mesh):
    return jax.shard_map(
        per_device,
        mesh=mesh,
        in_specs=(P("leaf", "rep"), P("leaf", None, None), P("leaf", None), P("leaf", "rep", None)),
        out_specs=(P("leaf", "rep", None), P("leaf", "rep", None)),
        check_vma=False,
    )
```

```python
import jax
import jax.numpy as jnp
from jax import lax
from jax.experimental import pallas as pl
from jax.experimental.pallas import tpu as pltpu
from jax.sharding import PartitionSpec as P

MESH = pl.DeviceIdType.MESH
Z, X, Y, CORES = 16, 4, 4, 2
PLANE = X * Y * CORES
GROUPS = 3
OWNER = (
    tuple((n // 3, n % 3, n % 3 + 1) for n in range(12)),
    ((0, 0, 0), (1, 0, 0), (3, 0, 0), (2, 0, 0), (0, 1, 0), (1, 2, 1), (1, 1, 0), (2, 1, 2), (2, 2, 3), (0, 2, 1), (3, 1, 2), (3, 2, 3)),
    ((0, 0, 2), (0, 1, 3), (3, 0, 0), (1, 0, 2), (1, 1, 3), (2, 0, 0), (2, 1, 1), (3, 1, 1), (1, 2, 0), (2, 2, 0), (3, 2, 0), (0, 2, 0)),
    tuple((n // 3, n % 3, n % 3 + 1) for n in range(12)),
)
SHIFT = ((1, 1, 1, 1), (0, 0, 2, 2), (0, 0, 0, 0))
PLACE = [[None] * 16 for _ in range(3)]
HELD = [[[None] * 3 for _ in range(X)] for _ in range(4)]
for kind in range(4):
    for n, (at_x, entry, steps) in enumerate(OWNER[kind]):
        block, row_group = divmod(12 * kind + n, 16)
        assert block == (3 * kind + entry) // 4 and steps == (3 * kind + entry + SHIFT[block][at_x]) % 4
        assert HELD[kind][at_x][entry] is None and 4 * steps + at_x not in PLACE[block]
        PLACE[block][row_group] = 4 * steps + at_x
        HELD[kind][at_x][entry] = n, steps
JUMPS = (3, -3, 0)
SPREAD = (
    (0, 1), (0, -1), (3, 3), (-3, -3), (1, 1), (-1, -1), (3, 1), (-3, -1), (3, 2), (-3, -2), (6, 1), (-6, -1), (6, 2),
)
STEPS = sorted({step for _, step in SPREAD} | {-step for _, step in SPREAD})
assert sorted({j % Z for j in JUMPS} | {(a + b) % Z for a, b in SPREAD}) == list(range(Z))
assert len(JUMPS) + len(SPREAD) == Z
TARGETS = sorted(
    ((dx, dy, dc) for dx in range(X) for dy in range(Y) for dc in range(CORES)),
    key=lambda d: (d == (0, 0, 0), -d[2], -min(d[0], X - d[0]) - min(d[1], Y - d[1])),
)
F32, BF16 = jnp.float32, jnp.bfloat16


def kernel(
    anc, struct_hbm, panels_hbm, inv_hbm, off, diag,
    struct_ref, panels, inv, pieces, st_send, st_all, st_smem, slots, tiles, stage, picked, lhs, placed, pt,
    d_send, d_recv,
    in_sem, s_sems, spread_send, z_recv, st_sems, pick_sems, d_send_sem, d_recv_sem,
):
    me, y = lax.axis_index("leaf"), lax.axis_index("rep")
    z, x, c = me // 8, (me // 2) % 4, me % 2

    def leaf(zz, xx, cc):
        return (zz * X + xx) * CORES + cc

    def along(step):
        return (z + Z + step) % Z

    def by(index, values):
        return sum(jnp.where(index == n, value, 0) for n, value in enumerate(values))

    shifts = [by(x, values) for values in SHIFT]
    owners = by(8 * (z % 4) + 2 * x + c, [
        sum((1 << 6 * j) * (o[0] + 4 * o[1] + 16 * o[2]) for j, o in enumerate(OWNER[kind][g // 2] for g in range(3 * n, 3 * n + 3)))
        for kind in range(4) for n in range(X * CORES)
    ])

    def sources(from_z):
        return by(4 * (from_z % 4) + x, [
            sum((1 << 6 * e) * (n + 16 * steps) for e, (n, steps) in enumerate(HELD[kind][at])) for kind in range(4) for at in range(X)
        ])

    get_panels = pltpu.make_async_copy(panels_hbm.at[0], panels, in_sem.at[0])
    get_inv = pltpu.make_async_copy(inv_hbm.at[0], inv, in_sem.at[1])
    get_struct = pltpu.make_async_copy(struct_hbm, struct_ref, in_sem.at[3])
    get_struct.start()
    get_panels.start()
    get_inv.start()

    barrier = pltpu.get_barrier_semaphore()

    def greet(n, carry):
        there = leaf(z, (x + n // 8) % X, (c + n % 2) % CORES)
        pl.semaphore_signal(barrier, inc=1, device_id=(there, (y + n // 2) % Y), device_id_type=MESH)
        return carry

    for jump in JUMPS:
        if jump:
            held = sources(along(-jump))
            for e in range(GROUPS):
                pair, steps = held // (1 << 6 * e) % 16, held // (1 << 6 * e + 4) % 4
                there = (leaf(along(-jump), pair // 3, (2 * pair + c) // 3 % 2), (y + Y - steps) % Y)
                pl.semaphore_signal(barrier, inc=1, device_id=there, device_id_type=MESH)
    for step in STEPS:
        pl.semaphore_signal(barrier, inc=1, device_id=(leaf(along(step), x, c), y), device_id_type=MESH)
    lax.fori_loop(1, PLANE, greet, 0)

    get_struct.wait()
    lane = lax.broadcasted_iota(jnp.int32, (8, 128), 1)
    blocks = jnp.zeros((8, 128), jnp.int32)
    for q in range(4):
        blocks = jnp.where(lane == q, struct_ref[0, q], blocks)
    slot = 2 * x + c
    st_send[...] = blocks
    st_all[slot] = blocks
    rows = anc[...].astype(F32)
    for h in range(3):
        for t in range(3):
            halves = [rows[8 * h:8 * h + 8, 256 * t + 128 * k:256 * t + 128 * k + 128] for k in range(2)]
            pieces[h, t] = jnp.concatenate(halves, axis=0).astype(BF16)

    pl.semaphore_wait(barrier, PLANE - 1 + GROUPS * (len(JUMPS) - 1) + len(STEPS))

    def tell(n, carry):
        pltpu.make_async_remote_copy(
            src_ref=st_send, dst_ref=st_all.at[slot], send_sem=st_sems.at[0], recv_sem=st_sems.at[1],
            device_id=(leaf(z, (x + n // 2) % X, (c + n % 2) % CORES), y), device_id_type=MESH,
        ).start()
        return carry

    def owner(j):
        one = owners // (1 << 6 * j) % 64
        return one // 4 % 4, one % 4, (y + one // 16) % Y, (3 * c + j) % 2

    def scatter(j, jump, here):
        entry, to_x, to_y, to_c = owner(j)
        landing = tiles.at[pl.ds(3 * (GROUPS * z + entry), 3)]
        if here:
            return pltpu.make_async_copy(pieces.at[j], landing, z_recv.at[0, entry])
        return pltpu.make_async_remote_copy(
            src_ref=pieces.at[j], dst_ref=landing,
            send_sem=s_sems.at[0] if jump else s_sems.at[1 + j], recv_sem=z_recv.at[jump % Z, entry],
            device_id=(leaf(along(jump), to_x, to_c), to_y), device_id_type=MESH,
        )

    def stays(j):
        _, to_x, to_y, to_c = owner(j)
        return jnp.logical_and(jnp.logical_and(to_x == x, to_y == y), to_c == c)

    for jump in JUMPS:
        for j in range(3):
            if jump:
                scatter(j, jump, False).start()
            else:
                pl.when(stays(j))(lambda: scatter(j, 0, True).start())
                pl.when(jnp.logical_not(stays(j)))(lambda: scatter(j, 0, False).start())
    lax.fori_loop(1, X * CORES, tell, 0)

    landed = set()

    def arrived(o, e):
        if (o, e) not in landed:
            landed.add((o, e))
            pltpu.make_async_copy(pieces.at[0], pieces.at[0], z_recv.at[o % Z, e]).wait()

    def pass_on(o, step, e):
        part = tiles.at[pl.ds(3 * (GROUPS * along(-o) + e), 3)]
        pltpu.make_async_remote_copy(
            src_ref=part, dst_ref=part, send_sem=spread_send, recv_sem=z_recv.at[(o + step) % Z, e],
            device_id=(leaf(along(step), x, c), y), device_id_type=MESH,
        ).start()

    for o, step in SPREAD:
        for e in range(GROUPS):
            if (o + step) % Z == Z // 2:
                arrived(o, e)
                arrived(-o, e)
                pl.when(c == 0)(lambda: pass_on(o, step, e))
                pl.when(c == 1)(lambda: pass_on(-o, -step, e))
            else:
                arrived(o, e)
                pass_on(o, step, e)
    get_panels.wait()
    pt[...] = panels[pl.ds(pl.multiple_of(256 * y, 256), 256), :].T
    told = st_all.at[pl.ds(0, X * CORES - 1)]
    pltpu.make_async_copy(told, told, st_sems.at[1]).wait()
    to_smem = pltpu.make_async_copy(st_all, st_smem, in_sem.at[2])
    to_smem.start()
    def target(n):
        dx, dy, dc = TARGETS[n]
        return (x + dx) % X, (y + dy) % Y, (c + dc) % CORES

    to_smem.wait()
    for n in range(PLANE):
        to_x, to_y, to_c = target(n)
        child = CORES * to_x + to_c
        row = st_smem[child, 0, to_y]
        shift = by(lax.rem(row, 3), shifts)
        for q in range(4):
            column = st_smem[child, 0, q]
            held = 4 * row + lax.rem(y + 8 - shift - lax.div(column, 3), 4)
            slots[n, q] = 3 * held + lax.rem(column, 3)
    for o in range(Z):
        o = o if o < Z // 2 else o - Z
        for e in range(GROUPS):
            arrived(o, e)

    def pick(n):
        for q in range(4):
            stage[n, q] = tiles[slots[n, q]]

    for n in range(PLANE - 1):
        pick(n)
        to_x, to_y, to_c = target(n)
        pltpu.make_async_remote_copy(
            src_ref=stage.at[n], dst_ref=picked.at[c, y, x], send_sem=pick_sems.at[0], recv_sem=pick_sems.at[1],
            device_id=(leaf(z, to_x, to_c), to_y), device_id_type=MESH,
        ).start()
    pick(PLANE - 1)
    pltpu.make_async_copy(stage.at[PLANE - 1], picked.at[c, y, x], pick_sems.at[1]).start()

    pltpu.make_async_copy(picked, picked, pick_sems.at[1]).wait()

    for q in range(4):
        quarter = lax.div(struct_ref[0, q], 3)
        for part in range(4):
            pair = [picked[k, lax.rem(quarter + part, 4), :, q].astype(F32).reshape(X, 2, 8, 128) for k in range(CORES)]
            for k in range(2):
                rows64 = jnp.concatenate([pair[0][:, k], pair[1][:, k]], axis=1).astype(BF16).reshape(64, 128)
                lhs[64 * part:64 * part + 64, 256 * q + 128 * k:256 * q + 128 * k + 128] = rows64
    update = (-jnp.dot(lhs[...], panels[...], preferred_element_type=F32)).astype(BF16)
    placed[...] = update.reshape(16, 16, 512)
    kind = lax.rem(by(y, [struct_ref[0, q] for q in range(4)]), 3)
    for first in range(0, 16, 4):
        places = by(kind, [sum(PLACE[n][first + m] << 4 * m for m in range(4)) for n in range(3)])
        for m in range(4):
            off[0, 16 * (first + m):16 * (first + m) + 16] = placed[lax.rem(lax.div(places, 1 << 4 * m), 16)]

    def share(row, count):
        return jnp.dot(pt[pl.ds(pl.multiple_of(row, count), count), :], off[0], preferred_element_type=F32)

    def give(j, half):
        rows = pl.ds(64 * half, 64)
        return pltpu.make_async_remote_copy(
            src_ref=d_send.at[j, rows], dst_ref=d_recv.at[j, rows],
            send_sem=d_send_sem.at[j, half], recv_sem=d_recv_sem.at[j, half],
            device_id=(me, (y + j + 1) % Y), device_id_type=MESH,
        )

    for half in range(2):
        for j in (1, 0, 2):
            row = 128 * ((y + j + 1) % Y) + 64 * half
            d_send[j, 64 * half:64 * half + 64] = share(row, 64).astype(BF16)
            give(j, half).start()
    get_inv.wait()
    diag[0] = inv[...] - share(128 * y, 128)
    for j in (0, 2, 1):
        for half in range(2):
            give(j, half).wait_recv()
        diag[0] -= d_recv[j].astype(F32)

    pltpu.make_async_copy(told, told, st_sems.at[0]).wait()
    for j in range(3):
        pl.when(jnp.logical_not(stays(j)))(lambda: scatter(j, 0, False).wait_send())
    jumped = tiles.at[pl.ds(0, 3 * GROUPS * (len(JUMPS) - 1))]
    pltpu.make_async_copy(jumped, jumped, s_sems.at[0]).wait()
    passed = tiles.at[pl.ds(0, 3 * GROUPS * len(SPREAD))]
    pltpu.make_async_copy(passed, passed, spread_send).wait()
    sent = stage.at[pl.ds(0, PLANE - 1)]
    pltpu.make_async_copy(sent, sent, pick_sems.at[0]).wait()
    for j in range(3):
        for half in range(2):
            give(j, half).wait_send()


def write_out(off, diag, off_hbm, diag_hbm, sems):
    put = [pltpu.make_async_copy(*pair) for pair in ((off, off_hbm, sems.at[0]), (diag, diag_hbm, sems.at[1]))]
    for copy in put:
        copy.start()
    for copy in put:
        copy.wait()


def per_device(ancestors, panels, structure, inverse_diag):
    vmem, smem, dma = pltpu.VMEM, pltpu.SMEM, pltpu.SemaphoreType.DMA
    results = pl.pallas_call(
        kernel,
        out_shape=(
            pltpu.VMEM((1, 256, 512), BF16),
            pltpu.VMEM((1, 128, 512), F32),
        ),
        in_specs=[
            pl.BlockSpec(memory_space=vmem),
            pl.BlockSpec(memory_space=pl.ANY),
            pl.BlockSpec(memory_space=pl.ANY),
            pl.BlockSpec(memory_space=pl.ANY),
        ],
        out_specs=(pl.BlockSpec(memory_space=vmem), pl.BlockSpec(memory_space=vmem)),
        scratch_shapes=[
            smem((1, 4), jnp.int32),
            vmem((1024, 512), BF16),
            vmem((128, 512), F32),
            vmem((3, 3, 16, 128), BF16),
            vmem((8, 128), jnp.int32),
            vmem((X * CORES, 8, 128), jnp.int32),
            smem((X * CORES, 8, 128), jnp.int32),
            smem((PLANE, 4), jnp.int32),
            vmem((GROUPS * Z * 3, 16, 128), BF16),
            vmem((PLANE, 4, 16, 128), BF16),
            vmem((CORES, Y, X, 4, 16, 128), BF16),
            vmem((256, 1024), BF16),
            vmem((16, 16, 512), BF16),
            vmem((512, 256), BF16),
            vmem((3, 128, 512), BF16),
            vmem((3, 128, 512), BF16),
            dma((4,)),
            dma((4,)),
            dma,
            dma((Z, GROUPS)),
            dma((2,)),
            dma((2,)),
            dma((3, 2)),
            dma((3, 2)),
        ],
        compiler_params=pltpu.CompilerParams(
            collective_id=0, has_side_effects=True, vmem_limit_bytes=32 * 1024 * 1024
        ),
    )(ancestors, *(pltpu.with_memory_space_constraint(a, pltpu.HBM) for a in (structure, panels, inverse_diag)))
    return pl.pallas_call(
        write_out,
        out_shape=(pltpu.HBM((1, 256, 512), BF16), pltpu.HBM((1, 128, 512), F32)),
        in_specs=[pl.BlockSpec(memory_space=vmem)] * 2,
        out_specs=(pl.BlockSpec(memory_space=pl.ANY),) * 2,
        scratch_shapes=[dma((2,))],
    )(*(pltpu.with_memory_space_constraint(a, pltpu.VMEM) for a in results))


def solution(mesh):
    return jax.shard_map(
        per_device,
        mesh=mesh,
        in_specs=(P("leaf", "rep"), P("leaf", None, None), P("leaf", None), P("leaf", "rep", None)),
        out_specs=(P("leaf", "rep", None), P("leaf", "rep", None)),
        check_vma=False,
    )
```

```python
import jax
import jax.numpy as jnp
from jax import lax
from jax.experimental import pallas as pl
from jax.experimental.pallas import tpu as pltpu
from jax.sharding import PartitionSpec as P

MESH = pl.DeviceIdType.MESH
Z, X, Y, CORES = 16, 4, 4, 2
PLANE = X * Y * CORES
GROUPS = 3
OWNER = (
    tuple((n // 3, n % 3, n % 3 + 1) for n in range(12)),
    ((0, 0, 0), (1, 0, 0), (3, 0, 0), (2, 0, 0), (0, 1, 0), (1, 2, 1), (1, 1, 0), (2, 1, 2), (2, 2, 3), (0, 2, 1), (3, 1, 2), (3, 2, 3)),
    ((0, 0, 2), (0, 1, 3), (3, 0, 0), (1, 0, 2), (1, 1, 3), (2, 0, 0), (2, 1, 1), (3, 1, 1), (1, 2, 0), (2, 2, 0), (3, 2, 0), (0, 2, 0)),
    tuple((n // 3, n % 3, n % 3 + 1) for n in range(12)),
)
SHIFT = ((1, 1, 1, 1), (0, 0, 2, 2), (0, 0, 0, 0))
PLACE = [[None] * 16 for _ in range(3)]
HELD = [[[None] * 3 for _ in range(X)] for _ in range(4)]
for kind in range(4):
    for n, (at_x, entry, steps) in enumerate(OWNER[kind]):
        block, row_group = divmod(12 * kind + n, 16)
        assert block == (3 * kind + entry) // 4 and steps == (3 * kind + entry + SHIFT[block][at_x]) % 4
        assert HELD[kind][at_x][entry] is None and 4 * steps + at_x not in PLACE[block]
        PLACE[block][row_group] = 4 * steps + at_x
        HELD[kind][at_x][entry] = n, steps
JUMPS = (3, -3, 0)
SPREAD = (
    (0, 1), (0, -1), (3, 3), (-3, -3), (1, 1), (-1, -1), (3, 1), (-3, -1), (3, 2), (-3, -2), (6, 1), (-6, -1), (6, 2),
)
STEPS = sorted({step for _, step in SPREAD} | {-step for _, step in SPREAD})
assert sorted({j % Z for j in JUMPS} | {(a + b) % Z for a, b in SPREAD}) == list(range(Z))
assert len(JUMPS) + len(SPREAD) == Z
TARGETS = sorted(
    ((dx, dy, dc) for dx in range(X) for dy in range(Y) for dc in range(CORES)),
    key=lambda d: (d == (0, 0, 0), -d[2], -min(d[0], X - d[0]) - min(d[1], Y - d[1])),
)
F32, BF16 = jnp.float32, jnp.bfloat16


def kernel(
    anc_hbm, struct_hbm, panels_hbm, inv_hbm, off, diag,
    struct_ref, panels, inv, pieces, st_send, st_all, st_smem, slots, tiles, stage, picked, lhs, placed, pt,
    d_send, d_recv,
    in_sem, s_sems, spread_send, z_recv, st_sems, pick_sems, d_send_sem, d_recv_sem,
):
    me, y = lax.axis_index("leaf"), lax.axis_index("rep")
    z, x, c = me // 8, (me // 2) % 4, me % 2

    def leaf(zz, xx, cc):
        return (zz * X + xx) * CORES + cc

    def along(step):
        return (z + Z + step) % Z

    def by(index, values):
        return sum(jnp.where(index == n, value, 0) for n, value in enumerate(values))

    shifts = [by(x, values) for values in SHIFT]
    owners = by(8 * (z % 4) + 2 * x + c, [
        sum((1 << 6 * j) * (o[0] + 4 * o[1] + 16 * o[2]) for j, o in enumerate(OWNER[kind][g // 2] for g in range(3 * n, 3 * n + 3)))
        for kind in range(4) for n in range(X * CORES)
    ])

    def sources(from_z):
        return by(4 * (from_z % 4) + x, [
            sum((1 << 6 * e) * (n + 16 * steps) for e, (n, steps) in enumerate(HELD[kind][at])) for kind in range(4) for at in range(X)
        ])

    get_anc = pltpu.make_async_copy(anc_hbm, pieces, in_sem.at[3])
    get_panels = pltpu.make_async_copy(panels_hbm.at[0], panels, in_sem.at[0])
    get_inv = pltpu.make_async_copy(inv_hbm.at[0], inv, in_sem.at[1])
    get_struct = pltpu.make_async_copy(struct_hbm, struct_ref, in_sem.at[4])
    get_anc.start()
    get_struct.start()
    get_panels.start()
    get_inv.start()

    barrier = pltpu.get_barrier_semaphore()

    def greet(n, carry):
        there = leaf(z, (x + n // 8) % X, (c + n % 2) % CORES)
        pl.semaphore_signal(barrier, inc=1, device_id=(there, (y + n // 2) % Y), device_id_type=MESH)
        return carry

    for jump in JUMPS:
        if jump:
            held = sources(along(-jump))
            for e in range(GROUPS):
                pair, steps = held // (1 << 6 * e) % 16, held // (1 << 6 * e + 4) % 4
                there = (leaf(along(-jump), pair // 3, (2 * pair + c) // 3 % 2), (y + Y - steps) % Y)
                pl.semaphore_signal(barrier, inc=1, device_id=there, device_id_type=MESH)
    for step in STEPS:
        pl.semaphore_signal(barrier, inc=1, device_id=(leaf(along(step), x, c), y), device_id_type=MESH)
    lax.fori_loop(1, PLANE, greet, 0)

    get_struct.wait()
    lane = lax.broadcasted_iota(jnp.int32, (8, 128), 1)
    blocks = jnp.zeros((8, 128), jnp.int32)
    for q in range(4):
        blocks = jnp.where(lane == q, struct_ref[0, q], blocks)
    slot = 2 * x + c
    st_send[...] = blocks
    st_all[slot] = blocks
    get_anc.wait()
    pl.semaphore_wait(barrier, PLANE - 1 + GROUPS * (len(JUMPS) - 1) + len(STEPS))

    def tell(n, carry):
        pltpu.make_async_remote_copy(
            src_ref=st_send, dst_ref=st_all.at[slot], send_sem=st_sems.at[0], recv_sem=st_sems.at[1],
            device_id=(leaf(z, (x + n // 2) % X, (c + n % 2) % CORES), y), device_id_type=MESH,
        ).start()
        return carry

    def owner(j):
        one = owners // (1 << 6 * j) % 64
        return one // 4 % 4, one % 4, (y + one // 16) % Y, (3 * c + j) % 2

    def scatter(j, jump, here):
        entry, to_x, to_y, to_c = owner(j)
        landing = tiles.at[pl.ds(3 * (GROUPS * z + entry), 3)]
        if here:
            return pltpu.make_async_copy(pieces.at[j], landing, z_recv.at[0, entry])
        return pltpu.make_async_remote_copy(
            src_ref=pieces.at[j], dst_ref=landing,
            send_sem=s_sems.at[0] if jump else s_sems.at[1 + j], recv_sem=z_recv.at[jump % Z, entry],
            device_id=(leaf(along(jump), to_x, to_c), to_y), device_id_type=MESH,
        )

    def stays(j):
        _, to_x, to_y, to_c = owner(j)
        return jnp.logical_and(jnp.logical_and(to_x == x, to_y == y), to_c == c)

    for jump in JUMPS:
        for j in range(3):
            if jump:
                scatter(j, jump, False).start()
            else:
                pl.when(stays(j))(lambda: scatter(j, 0, True).start())
                pl.when(jnp.logical_not(stays(j)))(lambda: scatter(j, 0, False).start())
    lax.fori_loop(1, X * CORES, tell, 0)

    landed = set()

    def arrived(o, e):
        if (o, e) not in landed:
            landed.add((o, e))
            pltpu.make_async_copy(pieces.at[0], pieces.at[0], z_recv.at[o % Z, e]).wait()

    def pass_on(o, step, e):
        part = tiles.at[pl.ds(3 * (GROUPS * along(-o) + e), 3)]
        pltpu.make_async_remote_copy(
            src_ref=part, dst_ref=part, send_sem=spread_send, recv_sem=z_recv.at[(o + step) % Z, e],
            device_id=(leaf(along(step), x, c), y), device_id_type=MESH,
        ).start()

    for o, step in SPREAD:
        for e in range(GROUPS):
            if (o + step) % Z == Z // 2:
                arrived(o, e)
                arrived(-o, e)
                pl.when(c == 0)(lambda: pass_on(o, step, e))
                pl.when(c == 1)(lambda: pass_on(-o, -step, e))
            else:
                arrived(o, e)
                pass_on(o, step, e)
    get_panels.wait()
    pt[...] = panels[pl.ds(pl.multiple_of(256 * y, 256), 256), :].T
    told = st_all.at[pl.ds(0, X * CORES - 1)]
    pltpu.make_async_copy(told, told, st_sems.at[1]).wait()
    to_smem = pltpu.make_async_copy(st_all, st_smem, in_sem.at[2])
    to_smem.start()
    def target(n):
        dx, dy, dc = TARGETS[n]
        return (x + dx) % X, (y + dy) % Y, (c + dc) % CORES

    to_smem.wait()
    for n in range(PLANE):
        to_x, to_y, to_c = target(n)
        child = CORES * to_x + to_c
        row = st_smem[child, 0, to_y]
        shift = by(lax.rem(row, 3), shifts)
        for q in range(4):
            column = st_smem[child, 0, q]
            held = 4 * row + lax.rem(y + 8 - shift - lax.div(column, 3), 4)
            slots[n, q] = 3 * held + lax.rem(column, 3)
    for o in range(Z):
        o = o if o < Z // 2 else o - Z
        for e in range(GROUPS):
            arrived(o, e)

    def pick(n):
        for q in range(4):
            stage[n, q] = tiles[slots[n, q]]

    for n in range(PLANE - 1):
        pick(n)
        to_x, to_y, to_c = target(n)
        pltpu.make_async_remote_copy(
            src_ref=stage.at[n], dst_ref=picked.at[c, y, x], send_sem=pick_sems.at[0], recv_sem=pick_sems.at[1],
            device_id=(leaf(z, to_x, to_c), to_y), device_id_type=MESH,
        ).start()
    pick(PLANE - 1)
    pltpu.make_async_copy(stage.at[PLANE - 1], picked.at[c, y, x], pick_sems.at[1]).start()

    pltpu.make_async_copy(picked, picked, pick_sems.at[1]).wait()

    for q in range(4):
        quarter = lax.div(struct_ref[0, q], 3)
        for part in range(4):
            pair = [picked[k, lax.rem(quarter + part, 4), :, q].astype(F32).reshape(X, 2, 8, 128) for k in range(CORES)]
            for k in range(2):
                rows64 = jnp.concatenate([pair[0][:, k], pair[1][:, k]], axis=1).astype(BF16).reshape(64, 128)
                lhs[64 * part:64 * part + 64, 256 * q + 128 * k:256 * q + 128 * k + 128] = rows64
    update = (-jnp.dot(lhs[...], panels[...], preferred_element_type=F32)).astype(BF16)
    placed[...] = update.reshape(16, 16, 512)
    kind = lax.rem(by(y, [struct_ref[0, q] for q in range(4)]), 3)
    for first in range(0, 16, 4):
        places = by(kind, [sum(PLACE[n][first + m] << 4 * m for m in range(4)) for n in range(3)])
        for m in range(4):
            off[0, 16 * (first + m):16 * (first + m) + 16] = placed[lax.rem(lax.div(places, 1 << 4 * m), 16)]

    def share(row, count):
        return jnp.dot(pt[pl.ds(pl.multiple_of(row, count), count), :], off[0], preferred_element_type=F32)

    def give(j, half):
        rows = pl.ds(64 * half, 64)
        return pltpu.make_async_remote_copy(
            src_ref=d_send.at[j, rows], dst_ref=d_recv.at[j, rows],
            send_sem=d_send_sem.at[j, half], recv_sem=d_recv_sem.at[j, half],
            device_id=(me, (y + j + 1) % Y), device_id_type=MESH,
        )

    for half in range(2):
        for j in (1, 0, 2):
            row = 128 * ((y + j + 1) % Y) + 64 * half
            d_send[j, 64 * half:64 * half + 64] = share(row, 64).astype(BF16)
            give(j, half).start()
    get_inv.wait()
    diag[0] = inv[...] - share(128 * y, 128)
    for j in (0, 2, 1):
        for half in range(2):
            give(j, half).wait_recv()
        diag[0] -= d_recv[j].astype(F32)

    pltpu.make_async_copy(told, told, st_sems.at[0]).wait()
    for j in range(3):
        pl.when(jnp.logical_not(stays(j)))(lambda: scatter(j, 0, False).wait_send())
    jumped = tiles.at[pl.ds(0, 3 * GROUPS * (len(JUMPS) - 1))]
    pltpu.make_async_copy(jumped, jumped, s_sems.at[0]).wait()
    passed = tiles.at[pl.ds(0, 3 * GROUPS * len(SPREAD))]
    pltpu.make_async_copy(passed, passed, spread_send).wait()
    sent = stage.at[pl.ds(0, PLANE - 1)]
    pltpu.make_async_copy(sent, sent, pick_sems.at[0]).wait()
    for j in range(3):
        for half in range(2):
            give(j, half).wait_send()


def write_out(off, diag, off_hbm, diag_hbm, sems):
    put = [pltpu.make_async_copy(*pair) for pair in ((off, off_hbm, sems.at[0]), (diag, diag_hbm, sems.at[1]))]
    for copy in put:
        copy.start()
    for copy in put:
        copy.wait()


def per_device(ancestors, panels, structure, inverse_diag):
    vmem, smem, dma = pltpu.VMEM, pltpu.SMEM, pltpu.SemaphoreType.DMA
    pieces = ancestors.reshape(3, 8, 3, 2, 128).transpose(0, 2, 3, 1, 4).reshape(3, 3, 16, 128)
    results = pl.pallas_call(
        kernel,
        out_shape=(
            pltpu.VMEM((1, 256, 512), BF16),
            pltpu.VMEM((1, 128, 512), F32),
        ),
        in_specs=[
            pl.BlockSpec(memory_space=pl.ANY),
            pl.BlockSpec(memory_space=pl.ANY),
            pl.BlockSpec(memory_space=pl.ANY),
            pl.BlockSpec(memory_space=pl.ANY),
        ],
        out_specs=(pl.BlockSpec(memory_space=vmem), pl.BlockSpec(memory_space=vmem)),
        scratch_shapes=[
            smem((1, 4), jnp.int32),
            vmem((1024, 512), BF16),
            vmem((128, 512), F32),
            vmem((3, 3, 16, 128), BF16),
            vmem((8, 128), jnp.int32),
            vmem((X * CORES, 8, 128), jnp.int32),
            smem((X * CORES, 8, 128), jnp.int32),
            smem((PLANE, 4), jnp.int32),
            vmem((GROUPS * Z * 3, 16, 128), BF16),
            vmem((PLANE, 4, 16, 128), BF16),
            vmem((CORES, Y, X, 4, 16, 128), BF16),
            vmem((256, 1024), BF16),
            vmem((16, 16, 512), BF16),
            vmem((512, 256), BF16),
            vmem((3, 128, 512), BF16),
            vmem((3, 128, 512), BF16),
            dma((5,)),
            dma((4,)),
            dma,
            dma((Z, GROUPS)),
            dma((2,)),
            dma((2,)),
            dma((3, 2)),
            dma((3, 2)),
        ],
        compiler_params=pltpu.CompilerParams(
            collective_id=0, has_side_effects=True, vmem_limit_bytes=32 * 1024 * 1024
        ),
    )(*(pltpu.with_memory_space_constraint(a, pltpu.HBM) for a in (pieces, structure, panels, inverse_diag)))
    return pl.pallas_call(
        write_out,
        out_shape=(pltpu.HBM((1, 256, 512), BF16), pltpu.HBM((1, 128, 512), F32)),
        in_specs=[pl.BlockSpec(memory_space=vmem)] * 2,
        out_specs=(pl.BlockSpec(memory_space=pl.ANY),) * 2,
        scratch_shapes=[dma((2,))],
    )(*(pltpu.with_memory_space_constraint(a, pltpu.VMEM) for a in results))


def solution(mesh):
    return jax.shard_map(
        per_device,
        mesh=mesh,
        in_specs=(P("leaf", "rep"), P("leaf", None, None), P("leaf", None), P("leaf", "rep", None)),
        out_specs=(P("leaf", "rep", None), P("leaf", "rep", None)),
        check_vma=False,
    )
```
